512 devices in a mesh: space: 128 (over z, y, core), mode: 4 (over x).
Axes of the slice: x: 4, y: 8, z: 8, core: 2. Of those that a mesh axis runs over, the one named last changes fastest.
Arguments:
- right_side: float32 [4, 2, 7, 262144], P('mode', None, None, 'space')
- jacobian: float32 [2, 7, 7, 7, 4096], P(None, None, None, None, 'space'), may hold values from -0.9 to 0.9
- neighbor_cols: int32 [6, 4096], P(None, 'space'), may hold values from 0 to 63
- halo_list: int32 [2048], P('space'), may hold values from 0 to 31
- iface_blocks: int32 [16384], P('space'), may hold values from 0 to 31
- iface_slot: int32 [16384], P('space'), may hold values from 0 to 255, as said below
- recv_target: int32 [32768], P('space'), may hold values from 0 to 32, as said below
- phase_map: int32 [4, 16384], P('mode', 'space'), may hold values from 0 to 35
- mortar: float32 [8192, 64], P('space'), may hold values from -0.75 to 0.75
Outputs:
- basis: float32 [4, 4, 2, 7, 262144], P(None, 'mode', None, None, 'space')
- hess: float32 [2, 4, 3], replicated
The draws below stay inside these ranges and needn't reach their ends.
Inputs may be any that keep to these rules, and one draw needn't show every extreme that they name: `iface_slot`: each device's rows name distinct slots, never of its own reader index; each device fills all 2 slots of one other reader device drawn from the seed, and at most 2 rows go from one device to one reader. `recv_target`: consistent with iface_slot: a slot that no row fills holds 32.
All inputs are finite; a program needn't handle non-finite values.
Results may differ from the reference program's by a relative error of at most 0.0005.
Values sent between devices are 32-bit elements; how exact they have to be, the bound alone decides.
A program may use at most 64 MiB of HBM per device.

```python
import math
import jax
import jax.numpy as jnp
from jax import lax

FIELDS = 7
BLK = 64
NBLK = 32
NNZ = 6
HB = 16
IR = 128
KRY = 3
NPHASE = 36
CAP = 2
NB = 4096
CELLS = 262144
N_SPACE = 128
N_MODE = 4


def draw_right_side(key, part):
    first = jax.random.fold_in(key, 0)
    shape = (N_MODE, 2, FIELDS, CELLS)
    device = (jnp.arange(CELLS) // (NBLK * BLK)).astype(jnp.float32)
    rise = 1.0 + 2.0 * device / max(N_SPACE - 1, 1)
    base = jax.random.normal(first, shape, jnp.float32)
    return (base * rise).astype(jnp.float32)


def interface_tables(key):
    count = N_SPACE
    others = (count - 2) * CAP

    def one(source):
        inner_key = jax.random.fold_in(key, source)
        key_a, key_b, key_c, key_d = jax.random.split(inner_key, 4)
        draw_pick = jax.random.randint(key_a, (), 0, count - 1)
        chosen = draw_pick + (draw_pick >= source).astype(jnp.int32)
        lower = jnp.minimum(source, chosen)
        upper = jnp.maximum(source, chosen)
        picks = jax.random.permutation(key_b, others)[:IR - CAP]
        readers = picks // CAP
        readers = readers + (readers >= lower).astype(jnp.int32)
        readers = readers + (readers >= upper).astype(jnp.int32)
        rest = readers * CAP + picks % CAP
        own = chosen * CAP + jnp.arange(CAP)
        slots = jnp.concatenate([own, rest])
        slots = slots[jax.random.permutation(key_c, IR)]
        targets = jax.random.randint(key_d, (IR,), 0, NBLK)
        return (slots.astype(jnp.int32), targets.astype(jnp.int32))
    slots, targets = jax.vmap(one)(jnp.arange(count))
    sources = jnp.broadcast_to(jnp.arange(count)[:, None], (count, IR))
    table = jnp.full((count, count, CAP), NBLK, jnp.int32)
    table = table.at[slots // CAP, sources, slots % CAP].set(targets)
    return (slots.reshape(-1), table.reshape(-1))


def draw_iface_slot(key, part):
    return interface_tables(key)[0]


def draw_recv_target(key, part):
    return interface_tables(key)[1]


def place_ends(entries, key, smallest, largest):
    place = [jax.random.randint(jax.random.fold_in(key, axis), (), 0, length) for axis, length in enumerate(entries.shape)]
    main_axis = entries.shape.index(max(entries.shape))
    next_to = place[:main_axis] + [(place[main_axis] + 1) % entries.shape[main_axis]] + place[main_axis + 1:]
    return entries.at[tuple(place)].set(smallest).at[tuple(next_to)].set(largest)


def block_levels(stream_key, shape, shards, smallest, largest):
    loudness, own = 1.0, jax.random.fold_in(stream_key, 6)
    for axis_at, shards_of in shards:
        steps = jnp.exp(jax.random.uniform(jax.random.fold_in(own, axis_at), (shards_of,), jnp.float32, smallest / len(shards), largest / len(shards)))
        loudness = loudness * jnp.repeat(steps, shape[axis_at] // shards_of).reshape([-1 if axis == axis_at else 1 for axis in range(len(shape))])
    return loudness


def gaussian(stream_key, extent, scale, bound, cuts=(), kind=jnp.bfloat16):
    values = jax.random.normal(stream_key, extent, jnp.float32) * scale
    if len(cuts) > 0:
        values = block_levels(stream_key, extent, cuts, -0.22, 0.18) * values
    return jnp.clip(values, min=-bound, max=bound).astype(kind)


def setup_inputs(seed: int = 0) -> dict:
    keys = jax.random.split(jax.random.key(seed), 10)
    return {
        "right_side": draw_right_side(jax.random.fold_in(keys[9], 71), 0),
        "jacobian": gaussian(keys[1], (2, FIELDS, FIELDS, NNZ + 1, NB), 0.15, 0.9, ((4, 128),), jnp.float32),
        "neighbor_cols": place_ends(jax.random.randint(keys[2], (NNZ, NB), 0, NBLK + 2 * HB), jax.random.fold_in(keys[2], 1), 0, (NBLK + 2 * HB) - 1).astype(jnp.int32),
        "halo_list": place_ends(jax.random.randint(keys[3], (N_SPACE * HB,), 0, NBLK), jax.random.fold_in(keys[3], 1), 0, NBLK - 1).astype(jnp.int32),
        "iface_blocks": place_ends(jax.random.randint(keys[4], (N_SPACE * IR,), 0, NBLK), jax.random.fold_in(keys[4], 1), 0, NBLK - 1).astype(jnp.int32),
        "iface_slot": draw_iface_slot(jax.random.fold_in(keys[9], 71), 0),
        "recv_target": draw_recv_target(jax.random.fold_in(keys[9], 71), 0),
        "phase_map": place_ends(jax.random.randint(keys[7], (N_MODE, N_SPACE * IR), 0, NPHASE), jax.random.fold_in(keys[7], 1), 0, NPHASE - 1).astype(jnp.int32),
        "mortar": gaussian(keys[8], (N_SPACE * BLK, BLK), BLK ** -0.5, 0.75, ((0, 128),), jnp.float32),
    }


HIGH = lax.Precision.HIGHEST
SHIFT = 2.0
OMEGA = 0.5
EPS = 1e-06

def apply_blocks(jacobian, gathered):
    real_part = jnp.einsum('oikb,ikbc->obc', jacobian[0], gathered[0], precision=HIGH) - jnp.einsum('oikb,ikbc->obc', jacobian[1], gathered[1], precision=HIGH)
    imag_part = jnp.einsum('oikb,ikbc->obc', jacobian[0], gathered[1], precision=HIGH) + jnp.einsum('oikb,ikbc->obc', jacobian[1], gathered[0], precision=HIGH)
    return jnp.stack([real_part, imag_part])

def shifted_self(level, blocks):
    omega = OMEGA * level
    return jnp.stack([SHIFT * blocks[0] - omega * blocks[1], SHIFT * blocks[1] + omega * blocks[0]])

def rotate_rows(level, offsets, rows):
    angle = level * offsets.astype(jnp.float32) * (2.0 * math.pi / NPHASE)
    cosine = jnp.cos(angle)[None, :, None]
    sine = jnp.sin(angle)[None, :, None]
    return jnp.stack([cosine * rows[0] - sine * rows[1], sine * rows[0] + cosine * rows[1]])

def reference(right_side, jacobian, neighbor_cols, halo_list, iface_blocks, iface_slot, recv_target, phase_map, mortar):
    total = NBLK * N_SPACE
    block_dev = jnp.arange(total, dtype=jnp.int32) // NBLK
    local = neighbor_cols
    own = block_dev * NBLK + local
    hprev = jnp.clip((block_dev - 1) * HB + local - NBLK, 0, N_SPACE * HB - 1)
    prev_blk = jnp.where(block_dev > 0, (block_dev - 1) * NBLK + halo_list[hprev], total)
    hnext = jnp.clip((block_dev + 1) * HB + local - NBLK - HB, 0, N_SPACE * HB - 1)
    next_blk = jnp.where(block_dev < N_SPACE - 1, (block_dev + 1) * NBLK + halo_list[hnext], total)
    glob = jnp.where(local < NBLK, own, jnp.where(local < NBLK + HB, prev_blk, next_blk))
    all_cols = jnp.concatenate([jnp.arange(total, dtype=jnp.int32)[None], glob.astype(jnp.int32)], 0)
    src_dev = jnp.arange(N_SPACE * IR, dtype=jnp.int32) // IR
    src_blk = src_dev * NBLK + iface_blocks
    reader = iface_slot // CAP
    target = recv_target[reader * (N_SPACE * CAP) + src_dev * CAP + iface_slot % CAP]
    dest_blk = jnp.where(target < NBLK, reader * NBLK + target, total).astype(jnp.int32)
    row_mortar = mortar.reshape(N_SPACE, BLK, BLK)[reader]
    count = jnp.float32(N_MODE * CELLS)

    def matvec(mode, field):
        level = jnp.float32(mode + 1)
        blocks = field.reshape(2, FIELDS, total, BLK)
        padded = jnp.concatenate([blocks, jnp.zeros((2, FIELDS, 1, BLK), jnp.float32)], 2)
        gathered = padded[:, :, all_cols, :]
        result = apply_blocks(jacobian, gathered) + shifted_self(level, blocks)
        turned = rotate_rows(level, phase_map[mode], blocks[:, :, src_blk, :])
        mortared = jnp.einsum('pfri,rij->pfrj', turned, row_mortar, precision=HIGH)
        added = jax.ops.segment_sum(jnp.moveaxis(mortared, 2, 0), dest_blk, num_segments=total + 1)[:total]
        result = result + jnp.moveaxis(added, 0, 2)
        return result.reshape(2, FIELDS, CELLS)

    def apply_all(field):
        return jnp.stack([matvec(mode, field[mode]) for mode in range(N_MODE)])

    def inner(left, right):
        real_part = jnp.sum(left[:, 0] * right[:, 0] + left[:, 1] * right[:, 1]) / count
        imag_part = jnp.sum(left[:, 0] * right[:, 1] - left[:, 1] * right[:, 0]) / count
        return (real_part, imag_part)
    first = jnp.sqrt(jnp.sum(right_side * right_side) / count + EPS)
    vectors = [right_side / first]
    hess = jnp.zeros((2, KRY + 1, KRY), jnp.float32)
    for step in range(KRY):
        image = apply_all(vectors[step])
        products = [inner(vector, image) for vector in vectors]
        for index, (real_part, imag_part) in enumerate(products):
            vector = vectors[index]
            image = image - jnp.stack([real_part * vector[:, 0] - imag_part * vector[:, 1], real_part * vector[:, 1] + imag_part * vector[:, 0]], 1)
            hess = hess.at[0, index, step].set(real_part).at[1, index, step].set(imag_part)
        length = jnp.sqrt(jnp.sum(image * image) / count + EPS)
        hess = hess.at[0, step + 1, step].set(length)
        vectors.append(image / length)
    return (jnp.stack(vectors), hess)
```

```python
import functools
import math

import jax
import jax.numpy as jnp
from jax import lax
from jax.experimental import pallas as pl
from jax.experimental.pallas import tpu as pltpu
from jax.sharding import PartitionSpec as P

MESH = pl.DeviceIdType.MESH
F32 = jnp.float32
BF16 = jnp.bfloat16
FIELDS = 7
BLK = 64
HB = 16
KRY = 3
NPHASE = 36
NBLK = 32
LANES = 128
SHIFT = 2.0
OMEGA = 0.5
EPS = 1e-06
CHUNKS = 4
STRIDE = 51
ROW = 16


def iota(shape, dim):
    return lax.broadcasted_iota(jnp.int32, shape, dim)


def split(x):
    hi = x.astype(BF16)
    return hi, (x - hi.astype(F32)).astype(BF16)


def matmul(a, b):
    return lax.dot_general(a, b, (((1,), (0,)), ((), ())), preferred_element_type=F32)


def matmul_nt(a, b):
    return lax.dot_general(a, b, (((1,), (1,)), ((), ())), preferred_element_type=F32)


def one_hot(mask):
    return jnp.where(mask, 1.0, 0.0)


def wide(x):
    return jnp.concatenate([x[k] for k in range(FIELDS)], axis=1)


def turn(x, sign):
    return pltpu.roll(x, BLK, axis=x.ndim - 1) * sign


def kernel(
    space,
    modes,
    field_ref,
    jac_ref,
    cols_ref,
    halo_ref,
    blocks_ref,
    slot_ref,
    target_ref,
    phase_ref,
    mortar_ref,
    out_ref,
    hess_ref,
    sbuf,
    rbuf,
    hsend,
    hrecv,
    first_buf,
    second_buf,
    coef,
    pmat,
    tmat,
    nmat,
    hmat,
    bdiag,
    image,
    a2a_send,
    a2a_recv,
    halo_send,
    halo_recv,
    red_send,
    red_recv,
):
    me = lax.axis_index("space")
    mode = lax.axis_index("mode")
    line = 16
    lines = space // line
    wide_group = lines * modes
    in_line = lax.rem(me, line)
    my_line = me // line
    in_wide = my_line * modes + mode
    chunk = space // CHUNKS
    count = float(space * modes * NBLK * BLK)

    def partner(i):
        return lax.rem(me + lax.rem(i * STRIDE, space), space)

    def line_partner(o):
        return {"space": my_line * line + lax.rem(in_line + o, line)}

    def wide_partner(o):
        there = lax.rem(in_wide + o, wide_group)
        return {"space": there // modes * line + in_line, "mode": lax.rem(there, modes)}

    barrier = pltpu.get_barrier_semaphore()

    def greet(i, c):
        pl.semaphore_signal(barrier, inc=1, device_id={"space": partner(i)}, device_id_type=MESH)
        return c

    def greet_wide(o, c):
        pl.semaphore_signal(barrier, inc=1, device_id=wide_partner(o), device_id_type=MESH)
        return c

    lax.fori_loop(1, space, greet, 0)
    lax.fori_loop(1, wide_group, greet_wide, 0)

    lane = iota((1, LANES), 1)
    sign = jnp.where(lane < BLK, -1.0, 1.0).astype(F32)
    level = (mode + 1).astype(F32)

    angle = phase_ref[...].astype(F32) * (level * (2.0 * math.pi / NPHASE))
    picked = one_hot(iota((NBLK, LANES), 0) == blocks_ref[...])
    turned = jnp.concatenate([picked * jnp.cos(angle), picked * jnp.sin(angle)], axis=0)
    t_hi, t_lo = split(turned)
    for c in range(CHUNKS):
        row = iota((2 * chunk, 1), 0)
        reader = partner(c * chunk + lax.rem(row, chunk))
        chosen = one_hot(slot_ref[...] == reader * 2 + row // chunk).astype(BF16)
        p_hi = matmul_nt(chosen, t_hi).astype(BF16)
        p_lo = matmul_nt(chosen, t_lo).astype(BF16)
        pmat[c] = jnp.concatenate([p_hi, p_lo, p_hi], axis=1)
    eye = one_hot(iota((NBLK, NBLK), 0) == iota((NBLK, NBLK), 1)).astype(BF16)
    halo_t = one_hot(iota((NBLK, HB), 0) == halo_ref[...]).astype(BF16)
    eye_h = one_hot(iota((HB, HB), 0) == iota((HB, HB), 1)).astype(BF16)
    picks = matmul_nt(eye_h, halo_t).astype(BF16)
    hmat[...] = jnp.concatenate([picks, picks], axis=1)

    for t in range(KRY):
        rbuf[t, 0] = jnp.zeros((ROW, LANES), F32)

    pl.semaphore_wait(barrier, space - 1 + wide_group - 1)

    def send_halo(t, hi, lo):
        packed = matmul(hmat[...], jnp.concatenate([hi, lo], axis=0))
        for k in range(FIELDS):
            hsend[t, k] = packed[:, k * LANES : (k + 1) * LANES]
        for side in range(2):
            there = lax.rem(me + (1 if side == 0 else space - 1), space)
            pltpu.make_async_remote_copy(
                hsend.at[t],
                hrecv.at[t, side],
                halo_send.at[t, side],
                halo_recv.at[t, side],
                device_id={"space": there},
                device_id_type=MESH,
            ).start()

    def halo_copy(t, side, sem):
        return pltpu.make_async_copy(hsend.at[t], hrecv.at[t, side], sem.at[t, side])

    def send_chunk(t, c, rows):
        packed = matmul(pmat[c], rows)
        flat = sbuf.at[t].reshape(space * ROW, LANES)
        for slot in range(2):
            for k in range(FIELDS):
                flat[pl.ds(c * chunk * ROW + slot * FIELDS + k, chunk, stride=ROW), :] = packed[
                    slot * chunk : (slot + 1) * chunk, k * LANES : (k + 1) * LANES
                ]

        def one(i, carry):
            pltpu.make_async_remote_copy(
                sbuf.at[t, i, pl.ds(0, 2 * FIELDS)],
                rbuf.at[t, i, pl.ds(0, 2 * FIELDS)],
                a2a_send.at[t, c],
                a2a_recv.at[t, c],
                device_id={"space": partner(i)},
                device_id_type=MESH,
            ).start()
            return carry

        lax.fori_loop(1 if c == 0 else c * chunk, (c + 1) * chunk, one, 0)

    def wait_chunk(t, c, sem):
        number = chunk - 1 if c == 0 else chunk
        part = rbuf.at[t, pl.ds(0, number), pl.ds(0, 2 * FIELDS)]
        pltpu.make_async_copy(part, part, sem.at[t, c]).wait()

    def start_sum(r, values):
        vector = jnp.zeros((1, LANES), F32)
        for n, value in enumerate(values):
            vector = jnp.where(lane == n, value, vector)
        first_buf[r, in_line] = vector

        def one(o, carry):
            pltpu.make_async_remote_copy(
                first_buf.at[r, in_line],
                first_buf.at[r, in_line],
                red_send.at[r, 0],
                red_recv.at[r, 0],
                device_id=line_partner(o),
                device_id_type=MESH,
            ).start()
            return carry

        lax.fori_loop(1, line, one, 0)

    def middle_sum(r):
        part = first_buf.at[r, pl.ds(0, line - 1)]
        pltpu.make_async_copy(part, part, red_recv.at[r, 0]).wait()
        second_buf[r, in_wide] = jnp.sum(first_buf[r], axis=0)

        def one(o, carry):
            pltpu.make_async_remote_copy(
                second_buf.at[r, in_wide],
                second_buf.at[r, in_wide],
                red_send.at[r, 1],
                red_recv.at[r, 1],
                device_id=wide_partner(o),
                device_id_type=MESH,
            ).start()
            return carry

        lax.fori_loop(1, wide_group, one, 0)

    def end_sum(r, number):
        part = second_buf.at[r, pl.ds(0, wide_group - 1)]
        pltpu.make_async_copy(part, part, red_recv.at[r, 1]).wait()
        total = jnp.sum(second_buf[r], axis=0) * (1.0 / count)
        return [
            jnp.sum(jnp.where(lane == n, total, 0.0), axis=1, keepdims=True) for n in range(number)
        ]

    def total(x):
        return jnp.sum(jnp.sum(jnp.sum(x, axis=0), axis=0, keepdims=True), axis=1, keepdims=True)

    def inner(left, right):
        return [total(left * right), total(turn(left, sign) * right)]

    def minus(field, factor, vector):
        return field - factor[0] * vector - factor[1] * turn(vector, sign)

    def prepare():
        ones = jnp.ones((1, LANES), F32)
        for h in range(2):
            part = jac_ref[:, h, :]
            hi = part.astype(BF16)
            mid = (part - hi.astype(F32)).astype(BF16)
            low = (part - hi.astype(F32) - mid.astype(F32)).astype(BF16)
            columns = matmul_nt(eye, hi) + matmul_nt(eye, mid) + matmul_nt(eye, low)
            for o in range(FIELDS):
                for i in range(FIELDS):
                    for j in range(FIELDS):
                        q = (o * FIELDS + i) * FIELDS + j
                        value = columns[:, q : q + 1]
                        if j == 0 and o == i:
                            value = value + (SHIFT if h == 0 else OMEGA * level)
                        coef[q, h] = value * (ones if h == 0 else sign)
        for j in range(FIELDS - 1):
            source = one_hot(iota((2 * NBLK, NBLK), 0) == cols_ref[j : j + 1, :]).astype(BF16)
            there = matmul_nt(eye, source).astype(BF16)
            nmat[j * NBLK : (j + 1) * NBLK, :] = jnp.concatenate([there, there], axis=1)
        block = one_hot(iota((NBLK, 2 * space), 0) == target_ref[...]).astype(BF16)
        for c in range(CHUNKS):
            row = iota((2 * chunk, 1), 0)
            index = lax.rem((c * chunk + lax.rem(row, chunk)) * STRIDE, space)
            writer = lax.rem(me + space - index, space)
            pick = one_hot(iota((2 * chunk, 2 * space), 1) == writer * 2 + row // chunk)
            there = matmul_nt(block, pick.astype(BF16)).astype(BF16)
            tmat[c] = jnp.concatenate([there, there], axis=1)
        bdiag[...] = jnp.zeros((LANES, LANES), F32)
        bdiag[0:BLK, 0:BLK] = mortar_ref[...]
        bdiag[BLK:LANES, BLK:LANES] = mortar_ref[...]

    def flux(t, field, hi, lo):
        sides = []
        for side in range(2):
            halo_copy(t, side, halo_recv).wait()
            there = wide(hrecv[t, side])
            edge = (me > 0) if side == 0 else (me < space - 1)
            sides.append(split(jnp.where(edge, there, 0.0)))
        sources = jnp.concatenate(
            [hi, sides[0][0], sides[1][0], lo, sides[0][1], sides[1][1]], axis=0
        )
        gathered = matmul(nmat[...], sources)
        for k in range(FIELDS):
            image[0, k] = field[k]
            for j in range(FIELDS - 1):
                image[j + 1, k] = gathered[j * NBLK : (j + 1) * NBLK, k * LANES : (k + 1) * LANES]

        def one(n, totals):
            j = n // FIELDS
            i = lax.rem(n, FIELDS)
            value = image[j, i]
            other = pltpu.roll(value, BLK, axis=1)
            return tuple(
                totals[o]
                + coef[o * FIELDS * FIELDS + i * FIELDS + j, 0] * value
                + coef[o * FIELDS * FIELDS + i * FIELDS + j, 1] * other
                for o in range(FIELDS)
            )

        zero = jnp.zeros((NBLK, LANES), F32)
        return lax.fori_loop(0, FIELDS * FIELDS, one, (zero,) * FIELDS)

    def arrived(t):
        sums = jnp.zeros((NBLK, FIELDS * LANES), F32)
        flat = rbuf.at[t].reshape(space * ROW, LANES)
        for c in range(CHUNKS):
            wait_chunk(t, c, a2a_recv)
            rows = jnp.concatenate(
                [
                    jnp.concatenate(
                        [
                            flat[
                                pl.ds(c * chunk * ROW + slot * FIELDS + k, chunk, stride=ROW), :
                            ]
                            for k in range(FIELDS)
                        ],
                        axis=1,
                    )
                    for slot in range(2)
                ],
                axis=0,
            )
            hi, lo = split(rows)
            sums = sums + matmul(tmat[c], jnp.concatenate([hi, lo], axis=0))
        rows = jnp.concatenate(
            [sums[:, k * LANES : (k + 1) * LANES] for k in range(FIELDS)], axis=0
        )
        hi, lo = split(rows)
        m_hi, m_lo = split(bdiag[...])
        return matmul(hi, m_hi) + (matmul(lo, m_hi) + matmul(hi, m_lo))

    def step(t, field, reduce_ops):
        flatly = wide(field)
        hi, lo = split(flatly)
        send_halo(t, hi, lo)
        reduce_ops[0]()
        i_hi, i_lo = split(wide(turn(field, sign)))
        rows = jnp.concatenate([hi, i_hi, hi, i_hi, lo, i_lo], axis=0)
        for c in range(CHUNKS):
            send_chunk(t, c, rows)
            if c + 1 < len(reduce_ops):
                reduce_ops[c + 1]()
        if t == 0:
            prepare()
        totals = flux(t, field, hi, lo)
        mortared = arrived(t)
        return jnp.stack(
            [totals[k] + mortared[k * NBLK : (k + 1) * NBLK] for k in range(FIELDS)]
        )

    hess = []
    forcing = field_ref[...]
    state = {}

    def end_first():
        state["first"] = jnp.sqrt(end_sum(0, 1)[0] + EPS)

    image0 = step(
        0,
        forcing,
        [
            lambda: start_sum(0, [total(forcing * forcing)]),
            lambda: middle_sum(0),
            lambda: None,
            end_first,
        ],
    )
    first = state["first"]
    out_ref[0] = forcing / first
    images = [jnp.where(first < jnp.inf, image0 / first, 0.0)]
    vectors = 1

    for t in range(1, KRY + 1):
        w = images[t - 1]

        def start_products(t=t, w=w):
            products = []
            for index in range(t):
                products += inner(out_ref[index], w)
            start_sum(2 * t - 1, products)

        def end_products(t=t, w=w):
            values = end_sum(2 * t - 1, 2 * t)
            factors = [(values[2 * n], values[2 * n + 1]) for n in range(t)]
            rest = w
            for index in range(t):
                rest = minus(rest, factors[index], out_ref[index])
            out_ref[t] = rest
            state["factors"] = factors
            start_sum(2 * t, [total(rest * rest)])

        def end_norm(t=t):
            length = jnp.sqrt(end_sum(2 * t, 1)[0] + EPS)
            state["length"] = length
            out_ref[t] = out_ref[t] / length

        middle = [
            lambda t=t: middle_sum(2 * t - 1),
            end_products,
            lambda t=t: middle_sum(2 * t),
        ]
        if t < KRY:
            plain = step(t, w, [start_products] + middle + [end_norm])
        else:
            for op in [start_products] + middle + [end_norm]:
                op()
        factors, length = state["factors"], state["length"]
        hess.append((factors, length))
        if t < KRY:
            for index in range(t):
                plain = minus(plain, factors[index], images[index])
            images.append(plain / length)

    row = iota((8, LANES), 0)
    column = iota((8, LANES), 1)
    table = jnp.zeros((8, LANES), F32)
    for j, (factors, length) in enumerate(hess):
        for index, factor in enumerate(factors):
            for part in range(2):
                table = jnp.where((row == part * 4 + index) & (column == j), factor[part], table)
        table = jnp.where((row == j + 1) & (column == j), length, table)
    hess_ref[...] = table

    for t in range(KRY):
        for side in range(2):
            halo_copy(t, side, halo_send).wait()
        for c in range(CHUNKS):
            wait_chunk(t, c, a2a_send)
    for r in range(2 * KRY + 1):
        part = first_buf.at[r, pl.ds(0, line - 1)]
        pltpu.make_async_copy(part, part, red_send.at[r, 0]).wait()
        part = second_buf.at[r, pl.ds(0, wide_group - 1)]
        pltpu.make_async_copy(part, part, red_send.at[r, 1]).wait()


def solution(mesh):
    space, modes = mesh.shape["space"], mesh.shape["mode"]
    wide_group = space // 16 * modes
    sums = 2 * KRY + 1
    dma = pltpu.SemaphoreType.DMA

    def local(right, jac, cols, halo, blocks, slot, target, phase, mortar):
        field = right[0].reshape(2, FIELDS, NBLK, BLK).transpose(1, 2, 0, 3)
        field = field.reshape(FIELDS, NBLK, LANES)
        jac = jac.transpose(1, 2, 3, 0, 4).reshape(FIELDS**3, 2, NBLK)
        vmem = pl.BlockSpec(memory_space=pltpu.VMEM)
        basis, table = pl.pallas_call(
            functools.partial(kernel, space, modes),
            out_shape=(
                jax.ShapeDtypeStruct((KRY + 1, FIELDS, NBLK, LANES), F32),
                jax.ShapeDtypeStruct((8, LANES), F32),
            ),
            in_specs=[vmem] * 9,
            out_specs=(vmem, vmem),
            scratch_shapes=[
                pltpu.VMEM((KRY, space, ROW, LANES), F32),
                pltpu.VMEM((KRY, space, ROW, LANES), F32),
                pltpu.VMEM((KRY, FIELDS, HB, LANES), F32),
                pltpu.VMEM((KRY, 2, FIELDS, HB, LANES), F32),
                pltpu.VMEM((sums, 16, 1, LANES), F32),
                pltpu.VMEM((sums, wide_group, 1, LANES), F32),
                pltpu.VMEM((FIELDS**3, 2, NBLK, LANES), F32),
                pltpu.VMEM((CHUNKS, 2 * space // CHUNKS, 6 * NBLK), BF16),
                pltpu.VMEM((CHUNKS, NBLK, 4 * space // CHUNKS), BF16),
                pltpu.VMEM(((FIELDS - 1) * NBLK, 4 * NBLK), BF16),
                pltpu.VMEM((HB, 2 * NBLK), BF16),
                pltpu.VMEM((LANES, LANES), F32),
                pltpu.VMEM((FIELDS, FIELDS, NBLK, LANES), F32),
                dma((KRY, CHUNKS)),
                dma((KRY, CHUNKS)),
                dma((KRY, 2)),
                dma((KRY, 2)),
                dma((sums, 2)),
                dma((sums, 2)),
            ],
            compiler_params=pltpu.CompilerParams(
                collective_id=0, has_side_effects=True, vmem_limit_bytes=48 << 20
            ),
        )(
            field,
            jac,
            cols,
            halo.reshape(1, HB),
            blocks.reshape(1, LANES),
            slot.reshape(1, LANES),
            target.reshape(1, 2 * space),
            phase,
            mortar,
        )
        basis = basis.reshape(KRY + 1, FIELDS, NBLK, 2, BLK).transpose(0, 3, 1, 2, 4)
        basis = basis.reshape(KRY + 1, 1, 2, FIELDS, NBLK * BLK)
        return basis, table.reshape(2, KRY + 1, LANES)[:, :, :KRY]

    return jax.shard_map(
        local,
        mesh=mesh,
        in_specs=(
            P("mode", None, None, "space"),
            P(None, None, None, None, "space"),
            P(None, "space"),
            P("space"),
            P("space"),
            P("space"),
            P("space"),
            P("mode", "space"),
            P("space", None),
        ),
        out_specs=(P(None, "mode", None, None, "space"), P()),
        check_vma=False,
    )
```

```python
import functools
import math

import jax
import jax.numpy as jnp
import numpy as np
from jax import lax
from jax.experimental import pallas as pl
from jax.experimental.pallas import tpu as pltpu
from jax.sharding import PartitionSpec as P

MESH = pl.DeviceIdType.MESH
F32 = jnp.float32
BF16 = jnp.bfloat16
FIELDS = 7
BLK = 64
HB = 16
KRY = 3
NPHASE = 36
NBLK = 32
LANES = 128
SHIFT = 2.0
OMEGA = 0.5
EPS = 1e-06
CHUNKS = 4
LINE = 16
ROW = 16


def iota(shape, dim):
    return lax.broadcasted_iota(jnp.int32, shape, dim)


def split(x):
    hi = x.astype(BF16)
    return hi, (x - hi.astype(F32)).astype(BF16)


def matmul(a, b):
    return lax.dot_general(a, b, (((1,), (0,)), ((), ())), preferred_element_type=F32)


def matmul_nt(a, b):
    return lax.dot_general(a, b, (((1,), (1,)), ((), ())), preferred_element_type=F32)


def one_hot(mask):
    return jnp.where(mask, 1.0, 0.0)


def wide(x):
    return jnp.concatenate([x[k] for k in range(FIELDS)], axis=1)


def turn(x, sign):
    return pltpu.roll(x, BLK, axis=x.ndim - 1) * sign


def two_sum(a, b):
    total = a + b
    part = total - a
    return total, (a - (total - part)) + (b - part)


def halves(x):
    big = x * 4097.0
    high = big - (big - x)
    return high, x - high


def two_product(a, b):
    product = a[0] * b[0]
    error = ((a[1] * b[1] - product) + a[1] * b[2] + a[2] * b[1]) + a[2] * b[2]
    return product, error


def ring(d, n):
    return min(d, n - d)


def sequence(space):
    lines = space // LINE
    rows = LINE // 2
    every = [(z, y, c) for z in range(lines) for y in range(rows) for c in range(2)]
    mixed = [every[i * 51 % space] for i in range(1, space)]
    near = [o for o in mixed if o[0] == 0 or o[1:] == (0, 0)]
    other = [o for o in mixed if o not in near]

    def far(o):
        return -ring(o[0], lines) - ring(o[1], rows)

    return [(0, 0, 0)] + sorted(near, key=far) + sorted(other, key=far), len(near)


def kernel(
    space,
    modes,
    field_ref,
    jac_ref,
    cols_ref,
    halo_ref,
    blocks_ref,
    slot_ref,
    target_ref,
    phase_ref,
    mortar_ref,
    order_ref,
    out_ref,
    hess_ref,
    sbuf,
    rbuf,
    hsend,
    hrecv,
    first_buf,
    second_buf,
    coef,
    pmat,
    tmat,
    nmat,
    hmat,
    bdiag,
    image,
    vector,
    images,
    ready,
    a2a_send,
    a2a_recv,
    halo_send,
    halo_recv,
    red_send,
    red_recv,
):
    me = lax.axis_index("space")
    mode = lax.axis_index("mode")
    lines = space // LINE
    rows_y = LINE // 2
    wide_group = lines * modes
    in_line = lax.rem(me, LINE)
    my_line = me // LINE
    in_wide = my_line * modes + mode
    chunk = space // CHUNKS
    count = float(space * modes * NBLK * BLK)
    offsets, near = sequence(space)
    z_part = [lax.rem(my_line + d, lines) * LINE for d in range(lines)]
    y_part = [lax.rem(in_line // 2 + d, rows_y) * 2 for d in range(rows_y)]
    c_part = [lax.rem(in_line + d, 2) for d in range(2)]
    x_part = [lax.rem(mode + d, modes) for d in range(modes)]

    def partner(i):
        z, y, c = offsets[i]
        return {"space": z_part[z] + y_part[y] + c_part[c]}

    line_partners = [
        {"space": z_part[0] + y_part[y] + c_part[c]}
        for y, c in sorted(
            [(y, c) for y in range(rows_y) for c in range(2)][1:], key=lambda o: -ring(o[0], rows_y)
        )
    ]
    wide_partners = [
        {"space": z_part[z] + in_line, "mode": x_part[x]}
        for z, x in sorted(
            [(z, x) for z in range(lines) for x in range(modes)][1:],
            key=lambda o: -ring(o[0], lines) - ring(o[1], modes),
        )
    ]

    def shifted(code, way):
        z = lax.rem(my_line + lines + way * (code // LINE), lines)
        y = lax.rem(in_line // 2 + rows_y + way * lax.rem(code // 2, rows_y), rows_y)
        c = lax.rem(in_line + lax.rem(code, 2), 2)
        return z * LINE + y * 2 + c

    barrier = pltpu.get_barrier_semaphore()
    for there in wide_partners + line_partners:
        pl.semaphore_signal(barrier, inc=1, device_id=there, device_id_type=MESH)

    lane = iota((1, LANES), 1)
    sign = jnp.where(lane < BLK, -1.0, 1.0).astype(F32)
    level = (mode + 1).astype(F32)

    angle = phase_ref[...].astype(F32) * (level * (2.0 * math.pi / NPHASE))
    picked = one_hot(iota((NBLK, LANES), 0) == blocks_ref[...])
    turned = jnp.concatenate([picked * jnp.cos(angle), picked * jnp.sin(angle)], axis=0)
    t_hi, t_lo = split(turned)
    for c in range(CHUNKS):
        row = iota((2 * chunk, 1), 0)
        reader = shifted(order_ref[2 * c * chunk : 2 * (c + 1) * chunk, :], 1)
        chosen = one_hot(slot_ref[...] == reader * 2 + row // chunk).astype(BF16)
        p_hi = matmul_nt(chosen, t_hi).astype(BF16)
        p_lo = matmul_nt(chosen, t_lo).astype(BF16)
        pmat[c] = jnp.concatenate([p_hi, p_lo, p_hi], axis=1)
    eye = one_hot(iota((NBLK, NBLK), 0) == iota((NBLK, NBLK), 1)).astype(BF16)
    halo_t = one_hot(iota((NBLK, HB), 0) == halo_ref[...]).astype(BF16)
    eye_h = one_hot(iota((HB, HB), 0) == iota((HB, HB), 1)).astype(BF16)
    picks = matmul_nt(eye_h, halo_t).astype(BF16)
    hmat[...] = jnp.concatenate([picks, picks], axis=1)

    for t in range(KRY):
        rbuf[t, 0] = jnp.zeros((ROW, LANES), F32)

    pl.semaphore_wait(barrier, LINE - 1 + wide_group - 1)
    for z in range(1, lines):
        there = {"space": z_part[z] + in_line}
        pl.semaphore_signal(ready, inc=1, device_id=there, device_id_type=MESH)

    def send_halo(t, hi, lo):
        packed = matmul(hmat[...], jnp.concatenate([hi, lo], axis=0))
        for k in range(FIELDS):
            hsend[t, k] = packed[:, k * LANES : (k + 1) * LANES]
        for side in range(2):
            there = lax.rem(me + (1 if side == 0 else space - 1), space)
            pltpu.make_async_remote_copy(
                hsend.at[t],
                hrecv.at[t, side],
                halo_send.at[t, side],
                halo_recv.at[t, side],
                device_id={"space": there},
                device_id_type=MESH,
            ).start()

    def halo_copy(t, side, sem):
        return pltpu.make_async_copy(hsend.at[t], hrecv.at[t, side], sem.at[t, side])

    def send_chunk(t, c, rows):
        packed = matmul(pmat[c], rows)
        flat = sbuf.at[t].reshape(space * ROW, LANES)
        for slot in range(2):
            for k in range(FIELDS):
                flat[pl.ds(c * chunk * ROW + slot * FIELDS + k, chunk, stride=ROW), :] = packed[
                    slot * chunk : (slot + 1) * chunk, k * LANES : (k + 1) * LANES
                ]

        for i in range(max(1, c * chunk), (c + 1) * chunk):
            if t == 0 and i == near + 1:
                pl.semaphore_wait(ready, lines - 1)
            pltpu.make_async_remote_copy(
                sbuf.at[t, i, pl.ds(0, 2 * FIELDS)],
                rbuf.at[t, i, pl.ds(0, 2 * FIELDS)],
                a2a_send.at[t, c],
                a2a_recv.at[t, c],
                device_id=partner(i),
                device_id_type=MESH,
            ).start()

    def wait_chunk(t, c, sem):
        number = chunk - 1 if c == 0 else chunk
        part = rbuf.at[t, pl.ds(0, number), pl.ds(0, 2 * FIELDS)]
        pltpu.make_async_copy(part, part, sem.at[t, c]).wait()

    def start_sum(r, row):
        first_buf[r, in_line] = row
        for there in line_partners:
            pltpu.make_async_remote_copy(
                first_buf.at[r, in_line],
                first_buf.at[r, in_line],
                red_send.at[r, 0],
                red_recv.at[r, 0],
                device_id=there,
                device_id_type=MESH,
            ).start()

    def add_rows(rows):
        errors = jnp.zeros((1, LANES), F32)
        while rows.shape[0] > 1:
            half = rows.shape[0] // 2
            rows, error = two_sum(rows[:half], rows[half:])
            errors = errors + jnp.sum(error, axis=0)
        return jnp.where(lane < BLK, rows[0], rows[0] + pltpu.roll(errors, BLK, axis=1))

    def middle_sum(r):
        part = first_buf.at[r, pl.ds(0, LINE - 1)]
        pltpu.make_async_copy(part, part, red_recv.at[r, 0]).wait()
        second_buf[r, in_wide] = add_rows(first_buf[r])
        for there in wide_partners:
            pltpu.make_async_remote_copy(
                second_buf.at[r, in_wide],
                second_buf.at[r, in_wide],
                red_send.at[r, 1],
                red_recv.at[r, 1],
                device_id=there,
                device_id_type=MESH,
            ).start()

    def end_sum(r, number):
        part = second_buf.at[r, pl.ds(0, wide_group - 1)]
        pltpu.make_async_copy(part, part, red_recv.at[r, 1]).wait()
        row = add_rows(second_buf[r]) * (1.0 / count)

        def pick(n):
            return jnp.sum(jnp.where(lane == n, row, 0.0), axis=1, keepdims=True)

        return [(pick(n), pick(BLK + n)) for n in range(number)]

    def square_sum(x):
        value = jnp.sum(jnp.sum(jnp.sum(x * x, axis=0), axis=0, keepdims=True), axis=1, keepdims=True)
        return jnp.where(lane == 0, value, 0.0)

    def products(left_refs, right_ref, square):
        number = 2 * len(left_refs) + (1 if square else 0)
        zero = jnp.zeros((8, LANES), F32)

        def one(k, sums):
            sums = list(sums)
            for g in range(NBLK // 8):
                part = slice(g * 8, (g + 1) * 8)

                def parts(x):
                    return (x,) + halves(x)

                right = parts(right_ref[k, part, :])
                pairs = []
                for ref in left_refs:
                    left = ref[k, part, :]
                    pairs += [parts(left), parts(pltpu.roll(left, BLK, axis=1) * sign)]
                if square:
                    pairs.append(right)
                for n, left in enumerate(pairs):
                    value, error = two_product(left, right)
                    sums[2 * n], lost = two_sum(sums[2 * n], value)
                    sums[2 * n + 1] = sums[2 * n + 1] + (error + lost)
            return tuple(sums)

        sums = lax.fori_loop(0, FIELDS, one, (zero,) * (2 * number))
        return [(sums[2 * n], sums[2 * n + 1]) for n in range(number)]

    def fold(pair, axis, shift):
        value, lost = two_sum(pair[0], pltpu.roll(pair[0], shift, axis=axis))
        return value, pair[1] + pltpu.roll(pair[1], shift, axis=axis) + lost

    def packed_sums(pairs):
        sub = iota((8, LANES), 0)
        across = iota((8, LANES), 1)
        row = jnp.zeros((1, LANES), F32)
        for start in range(0, len(pairs), 8):
            merged = None
            for n, pair in enumerate(pairs[start : start + 8]):
                for shift in (4, 2, 1):
                    pair = fold(pair, 0, shift)
                if merged is None:
                    merged = pair
                else:
                    merged = tuple(jnp.where(sub == n, a, b) for a, b in zip(pair, merged))
            for shift in (64, 32, 16, 8, 4, 2, 1):
                merged = fold(merged, 1, shift)
            for n, part in enumerate(merged):
                here = jnp.where(across == sub + (start + n * BLK), part, 0.0)
                row = row + jnp.sum(here, axis=0, keepdims=True)
        return row

    def minus(field, factor, vector):
        return field - factor[0] * vector - factor[1] * turn(vector, sign)

    def prepare():
        ones = jnp.ones((1, LANES), F32)
        for h in range(2):
            part = jac_ref[:, h, :]
            hi = part.astype(BF16)
            mid = (part - hi.astype(F32)).astype(BF16)
            low = (part - hi.astype(F32) - mid.astype(F32)).astype(BF16)
            columns = matmul_nt(eye, hi) + matmul_nt(eye, mid) + matmul_nt(eye, low)
            for o in range(FIELDS):
                for i in range(FIELDS):
                    for j in range(FIELDS):
                        q = (o * FIELDS + i) * FIELDS + j
                        value = columns[:, q : q + 1]
                        if j == 0 and o == i:
                            value = value + (SHIFT if h == 0 else OMEGA * level)
                        coef[q, h] = value * (ones if h == 0 else sign)
        for j in range(FIELDS - 1):
            source = one_hot(iota((2 * NBLK, NBLK), 0) == cols_ref[j : j + 1, :]).astype(BF16)
            there = matmul_nt(eye, source).astype(BF16)
            nmat[j * NBLK : (j + 1) * NBLK, :] = jnp.concatenate([there, there], axis=1)
        block = one_hot(iota((NBLK, 2 * space), 0) == target_ref[...]).astype(BF16)
        for c in range(CHUNKS):
            row = iota((2 * chunk, 1), 0)
            writer = shifted(order_ref[2 * c * chunk : 2 * (c + 1) * chunk, :], -1)
            pick = one_hot(iota((2 * chunk, 2 * space), 1) == writer * 2 + row // chunk)
            there = matmul_nt(block, pick.astype(BF16)).astype(BF16)
            tmat[c] = jnp.concatenate([there, there], axis=1)
        bdiag[...] = jnp.zeros((LANES, LANES), F32)
        bdiag[0:BLK, 0:BLK] = mortar_ref[...]
        bdiag[BLK:LANES, BLK:LANES] = mortar_ref[...]

    def flux(t, field, hi, lo):
        sides = []
        for side in range(2):
            halo_copy(t, side, halo_recv).wait()
            there = wide(hrecv[t, side])
            edge = (me > 0) if side == 0 else (me < space - 1)
            sides.append(split(jnp.where(edge, there, 0.0)))
        sources = jnp.concatenate(
            [hi, sides[0][0], sides[1][0], lo, sides[0][1], sides[1][1]], axis=0
        )
        gathered = matmul(nmat[...], sources)
        for k in range(FIELDS):
            image[0, k] = field[k]
            for j in range(FIELDS - 1):
                image[j + 1, k] = gathered[j * NBLK : (j + 1) * NBLK, k * LANES : (k + 1) * LANES]

        def one(n, totals):
            j = n // FIELDS
            i = lax.rem(n, FIELDS)
            value = image[j, i]
            other = pltpu.roll(value, BLK, axis=1)
            return tuple(
                totals[o]
                + coef[o * FIELDS * FIELDS + i * FIELDS + j, 0] * value
                + coef[o * FIELDS * FIELDS + i * FIELDS + j, 1] * other
                for o in range(FIELDS)
            )

        zero = jnp.zeros((NBLK, LANES), F32)
        return lax.fori_loop(0, FIELDS * FIELDS, one, (zero,) * FIELDS)

    def arrived(t):
        sums = jnp.zeros((NBLK, FIELDS * LANES), F32)
        flat = rbuf.at[t].reshape(space * ROW, LANES)
        for c in range(CHUNKS):
            wait_chunk(t, c, a2a_recv)
            rows = jnp.concatenate(
                [
                    jnp.concatenate(
                        [
                            flat[
                                pl.ds(c * chunk * ROW + slot * FIELDS + k, chunk, stride=ROW), :
                            ]
                            for k in range(FIELDS)
                        ],
                        axis=1,
                    )
                    for slot in range(2)
                ],
                axis=0,
            )
            hi, lo = split(rows)
            sums = sums + matmul(tmat[c], jnp.concatenate([hi, lo], axis=0))
        rows = jnp.concatenate(
            [sums[:, k * LANES : (k + 1) * LANES] for k in range(FIELDS)], axis=0
        )
        hi, lo = split(rows)
        m_hi, m_lo = split(bdiag[...])
        return matmul(hi, m_hi) + (matmul(lo, m_hi) + matmul(hi, m_lo))

    def swap(x):
        other = pltpu.roll(x, BLK, axis=2)
        sub = iota((FIELDS, NBLK, LANES), 1)
        across = iota((FIELDS, NBLK, LANES), 2)
        even = lax.rem(sub, 2) == 0
        other = jnp.where(even, pltpu.roll(other, NBLK - 1, axis=1), pltpu.roll(other, 1, axis=1))
        return jnp.where(even == (across < BLK), x, other)

    def step(t, field, row_of_sums, then):
        hi, lo = split(wide(field))
        i_hi, i_lo = split(wide(turn(field, sign)))
        rows = jnp.concatenate([hi, i_hi, hi, i_hi, lo, i_lo], axis=0)
        send_chunk(t, 0, rows)
        start_sum(t, row_of_sums())
        send_halo(t, hi, lo)
        send_chunk(t, 1, rows)
        send_chunk(t, 2, rows)
        middle_sum(t)
        send_chunk(t, 3, rows)
        if t == 0:
            prepare()
        totals = flux(t, field, hi, lo)
        then()
        mortared = arrived(t)
        return jnp.stack(
            [totals[k] + mortared[k * NBLK : (k + 1) * NBLK] for k in range(FIELDS)]
        )

    hess = []
    gram = {}
    state = {}

    def gram_products(t):
        own = products([], vector.at[t], True)
        return own + (products([vector.at[i] for i in range(t)], vector.at[t], False) if t else [])

    def image_products(t):
        return products([vector.at[i] for i in range(t + 1)], images.at[t], True)

    def new_vector(t):
        number = 2 * (t + 1)
        sums = [two_sum(*pair) for pair in end_sum(t + 1, number + 2 + 2 * t)]
        gram[t, t] = (sums[number + 1][0] - 1.0) + sums[number + 1][1]
        for i in range(t):
            gram[i, t] = (sums[number + 2 + 2 * i][0], sums[number + 3 + 2 * i][0])
        value, lost = sums[number]
        factors = []
        for i in range(t + 1):
            for part in range(2):
                h, rest = sums[2 * i + part]
                whole = (h,) + halves(h)
                square, error = two_product(whole, whole)
                value, missed = two_sum(value, -square)
                lost = lost + (missed - error - 2.0 * h * rest + square * gram[i, i])
            factors.append((sums[2 * i][0], sums[2 * i + 1][0]))
        for k in range(t + 1):
            for i in range(k):
                (a, b), (c, d), (g, f) = factors[i], factors[k], gram[i, k]
                lost = lost + 2.0 * ((a * c + b * d) * g - (a * d - b * c) * f)
        length = jnp.sqrt(jnp.maximum(value + lost, 0.0) + EPS)
        rest = images[t]
        for i in range(t + 1):
            rest = minus(rest, factors[i], vector[i])
        hess.append((factors, length))
        return rest / length

    forcing = swap(field_ref[...])

    def first_vector():
        first = jnp.sqrt(end_sum(0, 1)[0][0] + EPS)
        state["first"] = first
        vector[0] = forcing / first
        out_ref[0] = swap(vector[0])
        state["gram"] = gram_products(0)

    plain = step(0, forcing, lambda: square_sum(forcing), first_vector)
    first = state["first"]
    images[0] = jnp.where(first < jnp.inf, plain / first, 0.0)

    for t in range(1, KRY):

        def sums(t=t):
            return packed_sums(image_products(t - 1) + state["gram"])

        def next_vector(t=t):
            vector[t] = new_vector(t - 1)
            out_ref[t] = swap(vector[t])
            state["gram"] = gram_products(t)

        plain = step(t, images[t - 1], sums, next_vector)
        factors, length = hess[t - 1]
        for i in range(t):
            plain = minus(plain, factors[i], images[i])
        images[t] = plain / length

    start_sum(KRY, packed_sums(image_products(KRY - 1) + state["gram"]))
    middle_sum(KRY)
    out_ref[KRY] = swap(new_vector(KRY - 1))

    row = iota((8, LANES), 0)
    column = iota((8, LANES), 1)
    table = jnp.zeros((8, LANES), F32)
    for j, (factors, length) in enumerate(hess):
        for index, factor in enumerate(factors):
            for part in range(2):
                table = jnp.where((row == part * 4 + index) & (column == j), factor[part], table)
        table = jnp.where((row == j + 1) & (column == j), length, table)
    hess_ref[...] = table

    for t in range(KRY):
        for side in range(2):
            halo_copy(t, side, halo_send).wait()
        for c in range(CHUNKS):
            wait_chunk(t, c, a2a_send)
    for r in range(KRY + 1):
        part = first_buf.at[r, pl.ds(0, LINE - 1)]
        pltpu.make_async_copy(part, part, red_send.at[r, 0]).wait()
        part = second_buf.at[r, pl.ds(0, wide_group - 1)]
        pltpu.make_async_copy(part, part, red_send.at[r, 1]).wait()


def solution(mesh):
    space, modes = mesh.shape["space"], mesh.shape["mode"]
    wide_group = space // LINE * modes
    sums = KRY + 1
    chunk = space // CHUNKS
    codes = np.array([(z * LINE + y * 2 + c) for z, y, c in sequence(space)[0]], np.int32)
    codes = np.repeat(codes.reshape(CHUNKS, 1, chunk), 2, axis=1).reshape(2 * space, 1)
    dma = pltpu.SemaphoreType.DMA

    def local(right, jac, cols, halo, blocks, slot, target, phase, mortar):
        field = right[0].reshape(2, FIELDS, NBLK // 2, LANES).transpose(1, 2, 0, 3)
        field = field.reshape(FIELDS, NBLK, LANES)
        jac = jac.transpose(1, 2, 3, 0, 4).reshape(FIELDS**3, 2, NBLK)
        vmem = pl.BlockSpec(memory_space=pltpu.VMEM)
        basis, table = pl.pallas_call(
            functools.partial(kernel, space, modes),
            out_shape=(
                jax.ShapeDtypeStruct((KRY + 1, FIELDS, NBLK, LANES), F32),
                jax.ShapeDtypeStruct((8, LANES), F32),
            ),
            in_specs=[vmem] * 10,
            out_specs=(vmem, vmem),
            scratch_shapes=[
                pltpu.VMEM((KRY, space, ROW, LANES), F32),
                pltpu.VMEM((KRY, space, ROW, LANES), F32),
                pltpu.VMEM((KRY, FIELDS, HB, LANES), F32),
                pltpu.VMEM((KRY, 2, FIELDS, HB, LANES), F32),
                pltpu.VMEM((sums, LINE, 1, LANES), F32),
                pltpu.VMEM((sums, wide_group, 1, LANES), F32),
                pltpu.VMEM((FIELDS**3, 2, NBLK, LANES), F32),
                pltpu.VMEM((CHUNKS, 2 * space // CHUNKS, 6 * NBLK), BF16),
                pltpu.VMEM((CHUNKS, NBLK, 4 * space // CHUNKS), BF16),
                pltpu.VMEM(((FIELDS - 1) * NBLK, 4 * NBLK), BF16),
                pltpu.VMEM((HB, 2 * NBLK), BF16),
                pltpu.VMEM((LANES, LANES), F32),
                pltpu.VMEM((FIELDS, FIELDS, NBLK, LANES), F32),
                pltpu.VMEM((KRY, FIELDS, NBLK, LANES), F32),
                pltpu.VMEM((KRY, FIELDS, NBLK, LANES), F32),
                pltpu.SemaphoreType.REGULAR,
                dma((KRY, CHUNKS)),
                dma((KRY, CHUNKS)),
                dma((KRY, 2)),
                dma((KRY, 2)),
                dma((sums, 2)),
                dma((sums, 2)),
            ],
            compiler_params=pltpu.CompilerParams(
                collective_id=0, has_side_effects=True, vmem_limit_bytes=48 << 20
            ),
        )(
            field,
            jac,
            cols,
            halo.reshape(1, HB),
            blocks.reshape(1, LANES),
            slot.reshape(1, LANES),
            target.reshape(1, 2 * space),
            phase,
            mortar,
            jnp.asarray(codes),
        )
        basis = basis.reshape(KRY + 1, FIELDS, NBLK // 2, 2, LANES).transpose(0, 3, 1, 2, 4)
        basis = basis.reshape(KRY + 1, 1, 2, FIELDS, NBLK * BLK)
        return basis, table.reshape(2, KRY + 1, LANES)[:, :, :KRY]

    return jax.shard_map(
        local,
        mesh=mesh,
        in_specs=(
            P("mode", None, None, "space"),
            P(None, None, None, None, "space"),
            P(None, "space"),
            P("space"),
            P("space"),
            P("space"),
            P("space"),
            P("mode", "space"),
            P("space", None),
        ),
        out_specs=(P(None, "mode", None, None, "space"), P()),
        check_vma=False,
    )
```

```python
import functools
import math

import jax
import jax.numpy as jnp
import numpy as np
from jax import lax
from jax.experimental import pallas as pl
from jax.experimental.pallas import tpu as pltpu
from jax.sharding import PartitionSpec as P

MESH = pl.DeviceIdType.MESH
F32 = jnp.float32
BF16 = jnp.bfloat16
FIELDS = 7
BLK = 64
HB = 16
KRY = 3
NPHASE = 36
NBLK = 32
LANES = 128
SHIFT = 2.0
OMEGA = 0.5
EPS = 1e-06
CHUNKS = 4
LINE = 16
ROW = 16


def iota(shape, dim):
    return lax.broadcasted_iota(jnp.int32, shape, dim)


def split(x):
    hi = x.astype(BF16)
    return hi, (x - hi.astype(F32)).astype(BF16)


def matmul(a, b):
    return lax.dot_general(a, b, (((1,), (0,)), ((), ())), preferred_element_type=F32)


def matmul_nt(a, b):
    return lax.dot_general(a, b, (((1,), (1,)), ((), ())), preferred_element_type=F32)


def one_hot(mask):
    return jnp.where(mask, 1.0, 0.0)


def wide(x):
    return jnp.concatenate([x[k] for k in range(FIELDS)], axis=1)


def turn(x, sign):
    return pltpu.roll(x, BLK, axis=x.ndim - 1) * sign


def two_sum(a, b):
    total = a + b
    part = total - a
    return total, (a - (total - part)) + (b - part)


def halves(x):
    big = x * 4097.0
    high = big - (big - x)
    return high, x - high


def two_product(a, b):
    product = a[0] * b[0]
    error = ((a[1] * b[1] - product) + a[1] * b[2] + a[2] * b[1]) + a[2] * b[2]
    return product, error


def ring(d, n):
    return min(d, n - d)


def sequence(space):
    lines = space // LINE
    rows = LINE // 2
    every = [(z, y, c) for z in range(lines) for y in range(rows) for c in range(2)]
    mixed = [every[i * 51 % space] for i in range(1, space)]
    return [(0, 0, 0)] + sorted(mixed, key=lambda o: -ring(o[0], lines) - ring(o[1], rows))


def kernel(
    space,
    modes,
    field_hbm,
    jac_hbm,
    cols_hbm,
    halo_hbm,
    blocks_hbm,
    slot_hbm,
    target_hbm,
    phase_hbm,
    mortar_hbm,
    order_hbm,
    out_ref,
    hess_ref,
    field_ref,
    jac_ref,
    cols_ref,
    halo_ref,
    blocks_ref,
    slot_ref,
    target_ref,
    phase_ref,
    mortar_ref,
    order_ref,
    in_sem,
    sbuf,
    rbuf,
    hsend,
    hrecv,
    first_buf,
    second_buf,
    coef,
    pmat,
    tmat,
    nmat,
    hmat,
    bdiag,
    image,
    own_part,
    vector,
    images,
    ready,
    a2a_send,
    a2a_recv,
    halo_send,
    halo_recv,
    red_send,
    red_recv,
):
    me = lax.axis_index("space")
    mode = lax.axis_index("mode")
    lines = space // LINE
    rows_y = LINE // 2
    wide_group = lines * modes
    in_line = lax.rem(me, LINE)
    my_line = me // LINE
    in_wide = my_line * modes + mode
    chunk = space // CHUNKS
    count = float(space * modes * NBLK * BLK)
    offsets = sequence(space)
    z_part = [lax.rem(my_line + d, lines) * LINE for d in range(lines)]
    y_part = [lax.rem(in_line // 2 + d, rows_y) * 2 for d in range(rows_y)]
    c_part = [lax.rem(in_line + d, 2) for d in range(2)]
    x_part = [lax.rem(mode + d, modes) for d in range(modes)]

    def partner(i):
        z, y, c = offsets[i]
        return {"space": z_part[z] + y_part[y] + c_part[c]}

    line_partners = [
        {"space": z_part[0] + y_part[y] + c_part[c]}
        for y, c in sorted(
            [(y, c) for y in range(rows_y) for c in range(2)][1:], key=lambda o: -ring(o[0], rows_y)
        )
    ]
    wide_partners = [
        {"space": z_part[z] + in_line, "mode": x_part[x]}
        for z, x in sorted(
            [(z, x) for z in range(lines) for x in range(modes)][1:],
            key=lambda o: -ring(o[0], lines) - ring(o[1], modes),
        )
    ]

    def shifted(code, way):
        z = lax.rem(my_line + lines + way * (code // LINE), lines)
        y = lax.rem(in_line // 2 + rows_y + way * lax.rem(code // 2, rows_y), rows_y)
        c = lax.rem(in_line + lax.rem(code, 2), 2)
        return z * LINE + y * 2 + c

    copies = [
        pltpu.make_async_copy(source, there, in_sem.at[n])
        for n, (source, there) in enumerate(
            [
                (slot_hbm, slot_ref),
                (blocks_hbm, blocks_ref),
                (phase_hbm, phase_ref),
                (order_hbm, order_ref),
                (halo_hbm, halo_ref),
                (field_hbm, field_ref),
                (cols_hbm, cols_ref),
                (target_hbm, target_ref),
                (mortar_hbm, mortar_ref),
                (jac_hbm, jac_ref),
            ]
        )
    ]
    for copy in copies:
        copy.start()

    barrier = pltpu.get_barrier_semaphore()
    for there in wide_partners + line_partners:
        pl.semaphore_signal(barrier, inc=1, device_id=there, device_id_type=MESH)

    lane = iota((1, LANES), 1)
    sign = jnp.where(lane < BLK, -1.0, 1.0).astype(F32)
    level = (mode + 1).astype(F32)

    for copy in copies[:5]:
        copy.wait()
    angle = phase_ref[...].astype(F32) * (level * (2.0 * math.pi / NPHASE))
    picked = one_hot(iota((NBLK, LANES), 0) == blocks_ref[...])
    turned = jnp.concatenate([picked * jnp.cos(angle), picked * jnp.sin(angle)], axis=0)
    t_hi, t_lo = split(turned)
    for c in range(CHUNKS):
        row = iota((2 * chunk, 1), 0)
        reader = shifted(order_ref[2 * c * chunk : 2 * (c + 1) * chunk, :], 1)
        chosen = one_hot(slot_ref[...] == reader * 2 + row // chunk).astype(BF16)
        p_hi = matmul_nt(chosen, t_hi).astype(BF16)
        p_lo = matmul_nt(chosen, t_lo).astype(BF16)
        pmat[c] = jnp.concatenate([p_hi, p_lo, p_hi], axis=1)
    eye = one_hot(iota((NBLK, NBLK), 0) == iota((NBLK, NBLK), 1)).astype(BF16)
    halo_t = one_hot(iota((NBLK, HB), 0) == halo_ref[...]).astype(BF16)
    eye_h = one_hot(iota((HB, HB), 0) == iota((HB, HB), 1)).astype(BF16)
    picks = matmul_nt(eye_h, halo_t).astype(BF16)
    hmat[...] = jnp.concatenate([picks, picks], axis=1)

    for t in range(KRY):
        rbuf[t, 0] = jnp.zeros((ROW, LANES), F32)

    def enter():
        pl.semaphore_wait(barrier, LINE - 1 + wide_group - 1)
        for z in range(1, lines):
            there = {"space": z_part[z] + in_line}
            pl.semaphore_signal(ready, inc=1, device_id=there, device_id_type=MESH)

    def send_halo(t, hi, lo):
        packed = matmul(hmat[...], jnp.concatenate([hi, lo], axis=0))
        for k in range(FIELDS):
            hsend[t, k] = packed[:, k * LANES : (k + 1) * LANES]
        for side in range(2):
            there = lax.rem(me + (1 if side == 0 else space - 1), space)
            pltpu.make_async_remote_copy(
                hsend.at[t],
                hrecv.at[t, side],
                halo_send.at[t, side],
                halo_recv.at[t, side],
                device_id={"space": there},
                device_id_type=MESH,
            ).start()

    def halo_copy(t, side, sem):
        return pltpu.make_async_copy(hsend.at[t], hrecv.at[t, side], sem.at[t, side])

    def pack(t, c, rows):
        packed = matmul(pmat[c], rows)
        flat = sbuf.at[t].reshape(space * ROW, LANES)
        for slot in range(2):
            for k in range(FIELDS):
                flat[pl.ds(c * chunk * ROW + slot * FIELDS + k, chunk, stride=ROW), :] = packed[
                    slot * chunk : (slot + 1) * chunk, k * LANES : (k + 1) * LANES
                ]

    def send(t, places):
        for i in places:
            pltpu.make_async_remote_copy(
                sbuf.at[t, i, pl.ds(0, 2 * FIELDS)],
                rbuf.at[t, i, pl.ds(0, 2 * FIELDS)],
                a2a_send.at[t, i // chunk],
                a2a_recv.at[t, i // chunk],
                device_id=partner(i),
                device_id_type=MESH,
            ).start()

    def wait_chunk(t, c, sem):
        number = chunk - 1 if c == 0 else chunk
        part = rbuf.at[t, pl.ds(0, number), pl.ds(0, 2 * FIELDS)]
        pltpu.make_async_copy(part, part, sem.at[t, c]).wait()

    def start_sum(r, row):
        first_buf[r, in_line] = row
        for there in line_partners:
            pltpu.make_async_remote_copy(
                first_buf.at[r, in_line],
                first_buf.at[r, in_line],
                red_send.at[r, 0],
                red_recv.at[r, 0],
                device_id=there,
                device_id_type=MESH,
            ).start()

    def add_rows(rows):
        errors = jnp.zeros((1, LANES), F32)
        while rows.shape[0] > 1:
            half = rows.shape[0] // 2
            rows, error = two_sum(rows[:half], rows[half:])
            errors = errors + jnp.sum(error, axis=0)
        return jnp.where(lane < BLK, rows[0], rows[0] + pltpu.roll(errors, BLK, axis=1))

    def middle_sum(r):
        part = first_buf.at[r, pl.ds(0, LINE - 1)]
        pltpu.make_async_copy(part, part, red_recv.at[r, 0]).wait()
        second_buf[r, in_wide] = add_rows(first_buf[r])
        for there in wide_partners:
            pltpu.make_async_remote_copy(
                second_buf.at[r, in_wide],
                second_buf.at[r, in_wide],
                red_send.at[r, 1],
                red_recv.at[r, 1],
                device_id=there,
                device_id_type=MESH,
            ).start()

    def end_sum(r, number):
        part = second_buf.at[r, pl.ds(0, wide_group - 1)]
        pltpu.make_async_copy(part, part, red_recv.at[r, 1]).wait()
        row = add_rows(second_buf[r]) * (1.0 / count)

        def pick(n):
            return jnp.sum(jnp.where(lane == n, row, 0.0), axis=1, keepdims=True)

        return [(pick(n), pick(BLK + n)) for n in range(number)]

    def square_sum(x):
        value = jnp.sum(jnp.sum(jnp.sum(x * x, axis=0), axis=0, keepdims=True), axis=1, keepdims=True)
        return jnp.where(lane == 0, value, 0.0)

    def products(left_refs, right_ref, square):
        number = 2 * len(left_refs) + (1 if square else 0)
        zero = jnp.zeros((8, LANES), F32)

        def one(k, sums):
            sums = list(sums)
            for g in range(NBLK // 8):
                part = slice(g * 8, (g + 1) * 8)

                def parts(x):
                    return (x,) + halves(x)

                right = parts(right_ref[k, part, :])
                pairs = []
                for ref in left_refs:
                    left = ref[k, part, :]
                    pairs += [parts(left), parts(pltpu.roll(left, BLK, axis=1) * sign)]
                if square:
                    pairs.append(right)
                for n, left in enumerate(pairs):
                    value, error = two_product(left, right)
                    sums[2 * n], lost = two_sum(sums[2 * n], value)
                    sums[2 * n + 1] = sums[2 * n + 1] + (error + lost)
            return tuple(sums)

        sums = lax.fori_loop(0, FIELDS, one, (zero,) * (2 * number))
        return [(sums[2 * n], sums[2 * n + 1]) for n in range(number)]

    def fold(pair, axis, shift):
        value, lost = two_sum(pair[0], pltpu.roll(pair[0], shift, axis=axis))
        return value, pair[1] + pltpu.roll(pair[1], shift, axis=axis) + lost

    def packed_sums(pairs):
        sub = iota((8, LANES), 0)
        across = iota((8, LANES), 1)
        row = jnp.zeros((1, LANES), F32)
        for start in range(0, len(pairs), 8):
            merged = None
            for n, pair in enumerate(pairs[start : start + 8]):
                for shift in (4, 2, 1):
                    pair = fold(pair, 0, shift)
                if merged is None:
                    merged = pair
                else:
                    merged = tuple(jnp.where(sub == n, a, b) for a, b in zip(pair, merged))
            for shift in (64, 32, 16, 8, 4, 2, 1):
                merged = fold(merged, 1, shift)
            for n, part in enumerate(merged):
                here = jnp.where(across == sub + (start + n * BLK), part, 0.0)
                row = row + jnp.sum(here, axis=0, keepdims=True)
        return row

    def minus(field, factor, vector):
        return field - factor[0] * vector - factor[1] * turn(vector, sign)

    def prepare():
        for copy in copies[6:]:
            copy.wait()
        ones = jnp.ones((1, LANES), F32)
        for h in range(2):
            part = jac_ref[:, h, :]
            hi = part.astype(BF16)
            mid = (part - hi.astype(F32)).astype(BF16)
            low = (part - hi.astype(F32) - mid.astype(F32)).astype(BF16)
            columns = matmul_nt(eye, hi) + matmul_nt(eye, mid) + matmul_nt(eye, low)
            for o in range(FIELDS):
                for i in range(FIELDS):
                    for j in range(FIELDS):
                        q = (o * FIELDS + i) * FIELDS + j
                        value = columns[:, q : q + 1]
                        if j == 0 and o == i:
                            value = value + (SHIFT if h == 0 else OMEGA * level)
                        value = value * (ones if h == 0 else sign)
                        for g in range(NBLK // 8):
                            coef[j, g, (i * FIELDS + o) * 2 + h] = value[g * 8 : (g + 1) * 8]
        for j in range(FIELDS - 1):
            source = one_hot(iota((2 * NBLK, NBLK), 0) == cols_ref[j : j + 1, :]).astype(BF16)
            there = matmul_nt(eye, source).astype(BF16)
            nmat[j * NBLK : (j + 1) * NBLK, :] = jnp.concatenate([there, there], axis=1)
        block = one_hot(iota((NBLK, 2 * space), 0) == target_ref[...]).astype(BF16)
        for c in range(CHUNKS):
            row = iota((2 * chunk, 1), 0)
            writer = shifted(order_ref[2 * c * chunk : 2 * (c + 1) * chunk, :], -1)
            pick = one_hot(iota((2 * chunk, 2 * space), 1) == writer * 2 + row // chunk)
            there = matmul_nt(block, pick.astype(BF16)).astype(BF16)
            tmat[c] = jnp.concatenate([there, there], axis=1)
        bdiag[...] = jnp.zeros((LANES, LANES), F32)
        bdiag[0:BLK, 0:BLK] = mortar_ref[...]
        bdiag[BLK:LANES, BLK:LANES] = mortar_ref[...]

    def flux(t, field, hi, lo):
        sides = []
        for side in range(2):
            halo_copy(t, side, halo_recv).wait()
            there = wide(hrecv[t, side])
            edge = (me > 0) if side == 0 else (me < space - 1)
            sides.append(split(jnp.where(edge, there, 0.0)))
        sources = jnp.concatenate(
            [hi, sides[0][0], sides[1][0], lo, sides[0][1], sides[1][1]], axis=0
        )
        gathered = matmul(nmat[...], sources)
        for k in range(FIELDS):
            tile = jnp.concatenate([field[k], gathered[:, k * LANES : (k + 1) * LANES]], axis=0)
            image[0, k] = tile
            image[1, k] = pltpu.roll(tile, BLK, axis=1)

        for g in range(NBLK // 8):

            def one(j, sums, g=g):
                sums = list(sums)
                here = pl.ds(pl.multiple_of(j * NBLK + g * 8, 8), 8)
                factor = coef.at[j, g]
                for i in range(FIELDS):
                    value = image[0, i, here, :]
                    other = image[1, i, here, :]
                    for o in range(FIELDS):
                        n = 2 * (i * FIELDS + o)
                        sums[o] = sums[o] + (factor[n] * value + factor[n + 1] * other)
                return tuple(sums)

            sums = lax.fori_loop(0, FIELDS, one, (jnp.zeros((8, LANES), F32),) * FIELDS)
            for o in range(FIELDS):
                own_part[o, g * 8 : (g + 1) * 8, :] = sums[o]

    def arrived(t, c):
        wait_chunk(t, c, a2a_recv)
        flat = rbuf.at[t].reshape(space * ROW, LANES)
        rows = jnp.concatenate(
            [
                jnp.concatenate(
                    [
                        flat[pl.ds(c * chunk * ROW + slot * FIELDS + k, chunk, stride=ROW), :]
                        for k in range(FIELDS)
                    ],
                    axis=1,
                )
                for slot in range(2)
            ],
            axis=0,
        )
        hi, lo = split(rows)
        return matmul(tmat[c], jnp.concatenate([hi, lo], axis=0))

    def mortared(sums):
        rows = jnp.concatenate(
            [sums[:, k * LANES : (k + 1) * LANES] for k in range(FIELDS)], axis=0
        )
        hi, lo = split(rows)
        m_hi, m_lo = split(bdiag[...])
        out = matmul(hi, m_hi) + (matmul(lo, m_hi) + matmul(hi, m_lo))
        return out.reshape(FIELDS, NBLK, LANES)

    def swap(x):
        other = pltpu.roll(x, BLK, axis=2)
        sub = iota((FIELDS, NBLK, LANES), 1)
        across = iota((FIELDS, NBLK, LANES), 2)
        even = lax.rem(sub, 2) == 0
        other = jnp.where(even, pltpu.roll(other, NBLK - 1, axis=1), pltpu.roll(other, 1, axis=1))
        return jnp.where(even == (across < BLK), x, other)

    def step(t, field, row_of_sums, then):
        hi, lo = split(wide(field))
        i_hi, i_lo = split(wide(turn(field, sign)))
        rows = jnp.concatenate([hi, i_hi, hi, i_hi, lo, i_lo], axis=0)
        if t == 0:
            for c in range(CHUNKS):
                pack(t, c, rows)
            row = row_of_sums()
            enter()
            start_sum(t, row)
            near = [i for i in range(1, space) if offsets[i][0] == 0 or offsets[i][1:] == (0, 0)]
            other = [i for i in range(1, space) if i not in near]
            send(t, near)
            pl.semaphore_wait(ready, lines - 1)
            send_halo(t, hi, lo)
            send(t, other[: space // 4])
            middle_sum(t)
            send(t, other[space // 4 :])
            prepare()
        else:
            pack(t, 0, rows)
            send(t, range(1, chunk))
            start_sum(t, row_of_sums())
            pack(t, 1, rows)
            send(t, range(chunk, 2 * chunk))
            send_halo(t, hi, lo)
            middle_sum(t)
            for c in range(2, CHUNKS):
                pack(t, c, rows)
                send(t, range(c * chunk, (c + 1) * chunk))
        flux(t, field, hi, lo)
        sums = arrived(t, 0) + arrived(t, 1)
        then()
        sums = sums + arrived(t, 2)
        sums = sums + arrived(t, 3)
        return own_part[...] + mortared(sums)

    hess = []
    gram = {}
    state = {}

    def gram_products(t):
        own = products([], vector.at[t], True)
        return own + (products([vector.at[i] for i in range(t)], vector.at[t], False) if t else [])

    def image_products(t):
        return products([vector.at[i] for i in range(t + 1)], images.at[t], True)

    def new_vector(t):
        number = 2 * (t + 1)
        sums = [two_sum(*pair) for pair in end_sum(t + 1, number + 2 + 2 * t)]
        gram[t, t] = (sums[number + 1][0] - 1.0) + sums[number + 1][1]
        for i in range(t):
            gram[i, t] = (sums[number + 2 + 2 * i][0], sums[number + 3 + 2 * i][0])
        value, lost = sums[number]
        factors = []
        for i in range(t + 1):
            for part in range(2):
                h, rest = sums[2 * i + part]
                whole = (h,) + halves(h)
                square, error = two_product(whole, whole)
                value, missed = two_sum(value, -square)
                lost = lost + (missed - error - 2.0 * h * rest + square * gram[i, i])
            factors.append((sums[2 * i][0], sums[2 * i + 1][0]))
        for k in range(t + 1):
            for i in range(k):
                (a, b), (c, d), (g, f) = factors[i], factors[k], gram[i, k]
                lost = lost + 2.0 * ((a * c + b * d) * g - (a * d - b * c) * f)
        length = jnp.sqrt(jnp.maximum(value + lost, 0.0) + EPS)
        rest = images[t]
        for i in range(t + 1):
            rest = minus(rest, factors[i], vector[i])
        hess.append((factors, length))
        return rest / length

    for copy in copies[5:6]:
        copy.wait()
    forcing = swap(field_ref[...])

    def first_vector():
        first = jnp.sqrt(end_sum(0, 1)[0][0] + EPS)
        state["first"] = first
        vector[0] = forcing / first
        state["gram"] = gram_products(0)

    plain = step(0, forcing, lambda: square_sum(forcing), first_vector)
    first = state["first"]
    images[0] = jnp.where(first < jnp.inf, plain / first, 0.0)

    for t in range(1, KRY):

        def sums(t=t):
            return packed_sums(image_products(t - 1) + state["gram"])

        def next_vector(t=t):
            vector[t] = new_vector(t - 1)
            state["gram"] = gram_products(t)

        plain = step(t, images[t - 1], sums, next_vector)
        factors, length = hess[t - 1]
        for i in range(t):
            plain = minus(plain, factors[i], images[i])
        images[t] = plain / length

    start_sum(KRY, packed_sums(image_products(KRY - 1) + state["gram"]))
    for t in range(KRY):
        out_ref[t] = swap(vector[t])
    middle_sum(KRY)
    out_ref[KRY] = swap(new_vector(KRY - 1))

    row = iota((8, LANES), 0)
    column = iota((8, LANES), 1)
    table = jnp.zeros((8, LANES), F32)
    for j, (factors, length) in enumerate(hess):
        for index, factor in enumerate(factors):
            for part in range(2):
                table = jnp.where((row == part * 4 + index) & (column == j), factor[part], table)
        table = jnp.where((row == j + 1) & (column == j), length, table)
    hess_ref[...] = table

    for t in range(KRY):
        for side in range(2):
            halo_copy(t, side, halo_send).wait()
        for c in range(CHUNKS):
            wait_chunk(t, c, a2a_send)
    for r in range(KRY + 1):
        part = first_buf.at[r, pl.ds(0, LINE - 1)]
        pltpu.make_async_copy(part, part, red_send.at[r, 0]).wait()
        part = second_buf.at[r, pl.ds(0, wide_group - 1)]
        pltpu.make_async_copy(part, part, red_send.at[r, 1]).wait()


def solution(mesh):
    space, modes = mesh.shape["space"], mesh.shape["mode"]
    wide_group = space // LINE * modes
    sums = KRY + 1
    chunk = space // CHUNKS
    codes = np.array([(z * LINE + y * 2 + c) for z, y, c in sequence(space)], np.int32)
    codes = np.repeat(codes.reshape(CHUNKS, 1, chunk), 2, axis=1).reshape(2 * space, 1)
    dma = pltpu.SemaphoreType.DMA

    def local(right, jac, cols, halo, blocks, slot, target, phase, mortar):
        field = right[0].reshape(2, FIELDS, NBLK // 2, LANES).transpose(1, 2, 0, 3)
        field = field.reshape(FIELDS, NBLK, LANES)
        jac = jac.transpose(1, 2, 3, 0, 4).reshape(FIELDS**3, 2, NBLK)
        vmem = pl.BlockSpec(memory_space=pltpu.VMEM)
        basis, table = pl.pallas_call(
            functools.partial(kernel, space, modes),
            out_shape=(
                jax.ShapeDtypeStruct((KRY + 1, FIELDS, NBLK, LANES), F32),
                jax.ShapeDtypeStruct((8, LANES), F32),
            ),
            in_specs=[pl.BlockSpec(memory_space=pltpu.HBM)] * 10,
            out_specs=(vmem, vmem),
            scratch_shapes=[
                pltpu.VMEM((FIELDS, NBLK, LANES), F32),
                pltpu.VMEM((FIELDS**3, 2, NBLK), F32),
                pltpu.VMEM((FIELDS - 1, NBLK), jnp.int32),
                pltpu.VMEM((1, HB), jnp.int32),
                pltpu.VMEM((1, LANES), jnp.int32),
                pltpu.VMEM((1, LANES), jnp.int32),
                pltpu.VMEM((1, 2 * space), jnp.int32),
                pltpu.VMEM((1, LANES), jnp.int32),
                pltpu.VMEM((BLK, BLK), F32),
                pltpu.VMEM((2 * space, 1), jnp.int32),
                dma((10,)),
                pltpu.VMEM((KRY, space, ROW, LANES), F32),
                pltpu.VMEM((KRY, space, ROW, LANES), F32),
                pltpu.VMEM((KRY, FIELDS, HB, LANES), F32),
                pltpu.VMEM((KRY, 2, FIELDS, HB, LANES), F32),
                pltpu.VMEM((sums, LINE, 1, LANES), F32),
                pltpu.VMEM((sums, wide_group, 1, LANES), F32),
                pltpu.VMEM((FIELDS, NBLK // 8, 2 * FIELDS * FIELDS, 8, LANES), F32),
                pltpu.VMEM((CHUNKS, 2 * space // CHUNKS, 6 * NBLK), BF16),
                pltpu.VMEM((CHUNKS, NBLK, 4 * space // CHUNKS), BF16),
                pltpu.VMEM(((FIELDS - 1) * NBLK, 4 * NBLK), BF16),
                pltpu.VMEM((HB, 2 * NBLK), BF16),
                pltpu.VMEM((LANES, LANES), F32),
                pltpu.VMEM((2, FIELDS, FIELDS * NBLK, LANES), F32),
                pltpu.VMEM((FIELDS, NBLK, LANES), F32),
                pltpu.VMEM((KRY, FIELDS, NBLK, LANES), F32),
                pltpu.VMEM((KRY, FIELDS, NBLK, LANES), F32),
                pltpu.SemaphoreType.REGULAR,
                dma((KRY, CHUNKS)),
                dma((KRY, CHUNKS)),
                dma((KRY, 2)),
                dma((KRY, 2)),
                dma((sums, 2)),
                dma((sums, 2)),
            ],
            compiler_params=pltpu.CompilerParams(
                collective_id=0, has_side_effects=True, vmem_limit_bytes=64 << 20
            ),
        )(
            field,
            jac,
            cols,
            halo.reshape(1, HB),
            blocks.reshape(1, LANES),
            slot.reshape(1, LANES),
            target.reshape(1, 2 * space),
            phase,
            mortar,
            jnp.asarray(codes),
        )
        basis = basis.reshape(KRY + 1, FIELDS, NBLK // 2, 2, LANES).transpose(0, 3, 1, 2, 4)
        basis = basis.reshape(KRY + 1, 1, 2, FIELDS, NBLK * BLK)
        return basis, table.reshape(2, KRY + 1, LANES)[:, :, :KRY]

    return jax.shard_map(
        local,
        mesh=mesh,
        in_specs=(
            P("mode", None, None, "space"),
            P(None, None, None, None, "space"),
            P(None, "space"),
            P("space"),
            P("space"),
            P("space"),
            P("space"),
            P("mode", "space"),
            P("space", None),
        ),
        out_specs=(P(None, "mode", None, None, "space"), P()),
        check_vma=False,
    )
```

```python
import functools
import math

import jax
import jax.numpy as jnp
import numpy as np
from jax import lax
from jax.experimental import pallas as pl
from jax.experimental.pallas import tpu as pltpu
from jax.sharding import PartitionSpec as P

MESH = pl.DeviceIdType.MESH
F32 = jnp.float32
BF16 = jnp.bfloat16
FIELDS = 7
BLK = 64
HB = 16
KRY = 3
NPHASE = 36
NBLK = 32
LANES = 128
SHIFT = 2.0
OMEGA = 0.5
EPS = 1e-06
CHUNKS = 4
LINE = 16
ROW = 16


def iota(shape, dim):
    return lax.broadcasted_iota(jnp.int32, shape, dim)


def split(x):
    hi = x.astype(BF16)
    return hi, (x - hi.astype(F32)).astype(BF16)


def matmul(a, b):
    return lax.dot_general(a, b, (((1,), (0,)), ((), ())), preferred_element_type=F32)


def matmul_nt(a, b):
    return lax.dot_general(a, b, (((1,), (1,)), ((), ())), preferred_element_type=F32)


def one_hot(mask):
    return jnp.where(mask, 1.0, 0.0)


def wide(x):
    return jnp.concatenate([x[k] for k in range(FIELDS)], axis=1)


def turn(x, sign):
    return pltpu.roll(x, BLK, axis=x.ndim - 1) * sign


def two_sum(a, b):
    total = a + b
    part = total - a
    return total, (a - (total - part)) + (b - part)


def halves(x):
    big = x * 4097.0
    high = big - (big - x)
    return high, x - high


def two_product(a, b):
    product = a[0] * b[0]
    error = ((a[1] * b[1] - product) + a[1] * b[2] + a[2] * b[1]) + a[2] * b[2]
    return product, error


def ring(d, n):
    return min(d, n - d)


def sequence(space):
    lines = space // LINE
    rows = LINE // 2
    every = [(z, y, c) for z in range(lines) for y in range(rows) for c in range(2)]
    mixed = [every[i * 51 % space] for i in range(1, space)]
    return [(0, 0, 0)] + sorted(mixed, key=lambda o: -ring(o[0], lines) - ring(o[1], rows))


def kernel(
    space,
    modes,
    field_hbm,
    jac_hbm,
    cols_hbm,
    halo_hbm,
    blocks_hbm,
    slot_hbm,
    target_hbm,
    phase_hbm,
    mortar_hbm,
    order_hbm,
    out_ref,
    hess_ref,
    field_ref,
    jac_ref,
    cols_ref,
    halo_ref,
    blocks_ref,
    slot_ref,
    target_ref,
    phase_ref,
    mortar_ref,
    order_ref,
    in_sem,
    sbuf,
    rbuf,
    hsend,
    hrecv,
    first_buf,
    second_buf,
    coef,
    pmat,
    tmat,
    nmat,
    hmat,
    bdiag,
    image,
    own_part,
    vector,
    images,
    ready,
    a2a_send,
    a2a_recv,
    halo_send,
    halo_recv,
    red_send,
    red_recv,
):
    me = lax.axis_index("space")
    mode = lax.axis_index("mode")
    lines = space // LINE
    rows_y = LINE // 2
    wide_group = lines * modes
    in_line = lax.rem(me, LINE)
    my_line = me // LINE
    in_wide = my_line * modes + mode
    chunk = space // CHUNKS
    count = float(space * modes * NBLK * BLK)
    offsets = sequence(space)
    z_part = [lax.rem(my_line + d, lines) * LINE for d in range(lines)]
    y_part = [lax.rem(in_line // 2 + d, rows_y) * 2 for d in range(rows_y)]
    c_part = [lax.rem(in_line + d, 2) for d in range(2)]
    x_part = [lax.rem(mode + d, modes) for d in range(modes)]

    def partner(i):
        z, y, c = offsets[i]
        return {"space": z_part[z] + y_part[y] + c_part[c]}

    line_partners = [
        {"space": z_part[0] + y_part[y] + c_part[c]}
        for y, c in sorted(
            [(y, c) for y in range(rows_y) for c in range(2)][1:], key=lambda o: -ring(o[0], rows_y)
        )
    ]
    wide_partners = [
        {"space": z_part[z] + in_line, "mode": x_part[x]}
        for z, x in sorted(
            [(z, x) for z in range(lines) for x in range(modes)][1:],
            key=lambda o: -ring(o[0], lines) - ring(o[1], modes),
        )
    ]

    def shifted(code, way):
        z = lax.rem(my_line + lines + way * (code // LINE), lines)
        y = lax.rem(in_line // 2 + rows_y + way * lax.rem(code // 2, rows_y), rows_y)
        c = lax.rem(in_line + lax.rem(code, 2), 2)
        return z * LINE + y * 2 + c

    copies = [
        pltpu.make_async_copy(source, there, in_sem.at[n])
        for n, (source, there) in enumerate(
            [
                (slot_hbm, slot_ref),
                (blocks_hbm, blocks_ref),
                (phase_hbm, phase_ref),
                (order_hbm, order_ref),
                (halo_hbm, halo_ref),
                (field_hbm, field_ref),
                (cols_hbm, cols_ref),
                (target_hbm, target_ref),
                (mortar_hbm, mortar_ref),
                (jac_hbm, jac_ref),
            ]
        )
    ]
    barrier = pltpu.get_barrier_semaphore()
    for there in wide_partners + line_partners:
        pl.semaphore_signal(barrier, inc=1, device_id=there, device_id_type=MESH)
    for copy in copies:
        copy.start()

    lane = iota((1, LANES), 1)
    sign = jnp.where(lane < BLK, -1.0, 1.0).astype(F32)
    level = (mode + 1).astype(F32)

    for copy in copies[:5]:
        copy.wait()
    angle = phase_ref[...].astype(F32) * (level * (2.0 * math.pi / NPHASE))
    picked = one_hot(iota((NBLK, LANES), 0) == blocks_ref[...])
    turned = jnp.concatenate([picked * jnp.cos(angle), picked * jnp.sin(angle)], axis=0)
    t_hi, t_lo = split(turned)
    for c in range(CHUNKS):
        row = iota((2 * chunk, 1), 0)
        reader = shifted(order_ref[2 * c * chunk : 2 * (c + 1) * chunk, :], 1)
        chosen = one_hot(slot_ref[...] == reader * 2 + row // chunk).astype(BF16)
        p_hi = matmul_nt(chosen, t_hi).astype(BF16)
        p_lo = matmul_nt(chosen, t_lo).astype(BF16)
        pmat[c] = jnp.concatenate([p_hi, p_lo, p_hi], axis=1)
    eye = one_hot(iota((NBLK, NBLK), 0) == iota((NBLK, NBLK), 1)).astype(BF16)
    halo_t = one_hot(iota((NBLK, HB), 0) == halo_ref[...]).astype(BF16)
    eye_h = one_hot(iota((HB, HB), 0) == iota((HB, HB), 1)).astype(BF16)
    picks = matmul_nt(eye_h, halo_t).astype(BF16)
    hmat[...] = jnp.concatenate([picks, picks], axis=1)

    for t in range(KRY):
        rbuf[t, 0] = jnp.zeros((ROW, LANES), F32)

    def enter():
        pl.semaphore_wait(barrier, LINE - 1 + wide_group - 1)
        for z in range(1, lines):
            there = {"space": z_part[z] + in_line}
            pl.semaphore_signal(ready, inc=1, device_id=there, device_id_type=MESH)

    def send_halo(t, hi, lo):
        packed = matmul(hmat[...], jnp.concatenate([hi, lo], axis=0))
        for k in range(FIELDS):
            hsend[t, k] = packed[:, k * LANES : (k + 1) * LANES]
        for side in range(2):
            there = lax.rem(me + (1 if side == 0 else space - 1), space)
            pltpu.make_async_remote_copy(
                hsend.at[t],
                hrecv.at[t, side],
                halo_send.at[t, side],
                halo_recv.at[t, side],
                device_id={"space": there},
                device_id_type=MESH,
            ).start()

    def halo_copy(t, side, sem):
        return pltpu.make_async_copy(hsend.at[t], hrecv.at[t, side], sem.at[t, side])

    def pack(t, c, rows):
        packed = matmul(pmat[c], rows)
        flat = sbuf.at[t].reshape(space * ROW, LANES)
        for slot in range(2):
            for k in range(FIELDS):
                flat[pl.ds(c * chunk * ROW + slot * FIELDS + k, chunk, stride=ROW), :] = packed[
                    slot * chunk : (slot + 1) * chunk, k * LANES : (k + 1) * LANES
                ]

    def send(t, places):
        for i in places:
            pltpu.make_async_remote_copy(
                sbuf.at[t, i, pl.ds(0, 2 * FIELDS)],
                rbuf.at[t, i, pl.ds(0, 2 * FIELDS)],
                a2a_send.at[t, i // chunk],
                a2a_recv.at[t, i // chunk],
                device_id=partner(i),
                device_id_type=MESH,
            ).start()

    def wait_chunk(t, c, sem):
        number = chunk - 1 if c == 0 else chunk
        part = rbuf.at[t, pl.ds(0, number), pl.ds(0, 2 * FIELDS)]
        pltpu.make_async_copy(part, part, sem.at[t, c]).wait()

    def start_sum(r, row):
        first_buf[r, in_line] = row
        for there in line_partners:
            pltpu.make_async_remote_copy(
                first_buf.at[r, in_line],
                first_buf.at[r, in_line],
                red_send.at[r, 0],
                red_recv.at[r, 0],
                device_id=there,
                device_id_type=MESH,
            ).start()

    def add_rows(rows):
        errors = jnp.zeros((1, LANES), F32)
        while rows.shape[0] > 1:
            half = rows.shape[0] // 2
            rows, error = two_sum(rows[:half], rows[half:])
            errors = errors + jnp.sum(error, axis=0)
        return jnp.where(lane < BLK, rows[0], rows[0] + pltpu.roll(errors, BLK, axis=1))

    def middle_sum(r):
        part = first_buf.at[r, pl.ds(0, LINE - 1)]
        pltpu.make_async_copy(part, part, red_recv.at[r, 0]).wait()
        second_buf[r, in_wide] = add_rows(first_buf[r])
        for there in wide_partners:
            pltpu.make_async_remote_copy(
                second_buf.at[r, in_wide],
                second_buf.at[r, in_wide],
                red_send.at[r, 1],
                red_recv.at[r, 1],
                device_id=there,
                device_id_type=MESH,
            ).start()

    def end_sum(r, number):
        part = second_buf.at[r, pl.ds(0, wide_group - 1)]
        pltpu.make_async_copy(part, part, red_recv.at[r, 1]).wait()
        row = add_rows(second_buf[r]) * (1.0 / count)

        def pick(n):
            return jnp.sum(jnp.where(lane == n, row, 0.0), axis=1, keepdims=True)

        return [(pick(n), pick(BLK + n)) for n in range(number)]

    def square_sum(x):
        value = jnp.sum(jnp.sum(jnp.sum(x * x, axis=0), axis=0, keepdims=True), axis=1, keepdims=True)
        return jnp.where(lane == 0, value, 0.0)

    def products(left_refs, right_ref, square):
        number = 2 * len(left_refs) + (1 if square else 0)
        zero = jnp.zeros((8, LANES), F32)

        def one(k, sums):
            sums = list(sums)
            for g in range(NBLK // 8):
                part = slice(g * 8, (g + 1) * 8)

                def parts(x):
                    return (x,) + halves(x)

                right = parts(right_ref[k, part, :])
                pairs = []
                for ref in left_refs:
                    left = ref[k, part, :]
                    pairs += [parts(left), parts(pltpu.roll(left, BLK, axis=1) * sign)]
                if square:
                    pairs.append(right)
                for n, left in enumerate(pairs):
                    value, error = two_product(left, right)
                    sums[2 * n], lost = two_sum(sums[2 * n], value)
                    sums[2 * n + 1] = sums[2 * n + 1] + (error + lost)
            return tuple(sums)

        sums = lax.fori_loop(0, FIELDS, one, (zero,) * (2 * number))
        return [(sums[2 * n], sums[2 * n + 1]) for n in range(number)]

    def fold(pair, axis, shift):
        value, lost = two_sum(pair[0], pltpu.roll(pair[0], shift, axis=axis))
        return value, pair[1] + pltpu.roll(pair[1], shift, axis=axis) + lost

    def packed_sums(pairs):
        sub = iota((8, LANES), 0)
        across = iota((8, LANES), 1)
        row = jnp.zeros((1, LANES), F32)
        for start in range(0, len(pairs), 8):
            merged = None
            for n, pair in enumerate(pairs[start : start + 8]):
                for shift in (4, 2, 1):
                    pair = fold(pair, 0, shift)
                if merged is None:
                    merged = pair
                else:
                    merged = tuple(jnp.where(sub == n, a, b) for a, b in zip(pair, merged))
            for shift in (64, 32, 16, 8, 4, 2, 1):
                merged = fold(merged, 1, shift)
            for n, part in enumerate(merged):
                here = jnp.where(across == sub + (start + n * BLK), part, 0.0)
                row = row + jnp.sum(here, axis=0, keepdims=True)
        return row

    def minus(field, factor, vector):
        return field - factor[0] * vector - factor[1] * turn(vector, sign)

    def prepare():
        for copy in copies[6:]:
            copy.wait()
        ones = jnp.ones((1, LANES), F32)
        for h in range(2):
            part = jac_ref[:, h, :]
            hi = part.astype(BF16)
            mid = (part - hi.astype(F32)).astype(BF16)
            low = (part - hi.astype(F32) - mid.astype(F32)).astype(BF16)
            columns = matmul_nt(eye, hi) + matmul_nt(eye, mid) + matmul_nt(eye, low)
            for o in range(FIELDS):
                for i in range(FIELDS):
                    for j in range(FIELDS):
                        q = (o * FIELDS + i) * FIELDS + j
                        value = columns[:, q : q + 1]
                        if j == 0 and o == i:
                            value = value + (SHIFT if h == 0 else OMEGA * level)
                        value = value * (ones if h == 0 else sign)
                        for g in range(NBLK // 8):
                            coef[j, g, (i * FIELDS + o) * 2 + h] = value[g * 8 : (g + 1) * 8]
        for j in range(FIELDS - 1):
            source = one_hot(iota((2 * NBLK, NBLK), 0) == cols_ref[j : j + 1, :]).astype(BF16)
            there = matmul_nt(eye, source).astype(BF16)
            nmat[j * NBLK : (j + 1) * NBLK, :] = jnp.concatenate([there, there], axis=1)
        block = one_hot(iota((NBLK, 2 * space), 0) == target_ref[...]).astype(BF16)
        for c in range(CHUNKS):
            row = iota((2 * chunk, 1), 0)
            writer = shifted(order_ref[2 * c * chunk : 2 * (c + 1) * chunk, :], -1)
            pick = one_hot(iota((2 * chunk, 2 * space), 1) == writer * 2 + row // chunk)
            there = matmul_nt(block, pick.astype(BF16)).astype(BF16)
            tmat[c] = jnp.concatenate([there, there], axis=1)
        bdiag[...] = jnp.zeros((LANES, LANES), F32)
        bdiag[0:BLK, 0:BLK] = mortar_ref[...]
        bdiag[BLK:LANES, BLK:LANES] = mortar_ref[...]

    def flux(t, field, hi, lo):
        sides = []
        for side in range(2):
            halo_copy(t, side, halo_recv).wait()
            there = wide(hrecv[t, side])
            edge = (me > 0) if side == 0 else (me < space - 1)
            sides.append(split(jnp.where(edge, there, 0.0)))
        sources = jnp.concatenate(
            [hi, sides[0][0], sides[1][0], lo, sides[0][1], sides[1][1]], axis=0
        )
        gathered = matmul(nmat[...], sources)
        for k in range(FIELDS):
            tile = jnp.concatenate([field[k], gathered[:, k * LANES : (k + 1) * LANES]], axis=0)
            image[0, k] = tile
            image[1, k] = pltpu.roll(tile, BLK, axis=1)

        for g in range(NBLK // 8):

            def one(j, sums, g=g):
                sums = list(sums)
                here = pl.ds(pl.multiple_of(j * NBLK + g * 8, 8), 8)
                factor = coef.at[j, g]
                for i in range(FIELDS):
                    value = image[0, i, here, :]
                    other = image[1, i, here, :]
                    for o in range(FIELDS):
                        n = 2 * (i * FIELDS + o)
                        sums[o] = sums[o] + (factor[n] * value + factor[n + 1] * other)
                return tuple(sums)

            sums = lax.fori_loop(0, FIELDS, one, (jnp.zeros((8, LANES), F32),) * FIELDS)
            for o in range(FIELDS):
                own_part[o, g * 8 : (g + 1) * 8, :] = sums[o]

    def arrived(t, c):
        wait_chunk(t, c, a2a_recv)
        flat = rbuf.at[t].reshape(space * ROW, LANES)
        rows = jnp.concatenate(
            [
                jnp.concatenate(
                    [
                        flat[pl.ds(c * chunk * ROW + slot * FIELDS + k, chunk, stride=ROW), :]
                        for k in range(FIELDS)
                    ],
                    axis=1,
                )
                for slot in range(2)
            ],
            axis=0,
        )
        hi, lo = split(rows)
        return matmul(tmat[c], jnp.concatenate([hi, lo], axis=0))

    def mortared(sums):
        rows = jnp.concatenate(
            [sums[:, k * LANES : (k + 1) * LANES] for k in range(FIELDS)], axis=0
        )
        hi, lo = split(rows)
        m_hi, m_lo = split(bdiag[...])
        out = matmul(hi, m_hi) + (matmul(lo, m_hi) + matmul(hi, m_lo))
        return out.reshape(FIELDS, NBLK, LANES)

    def swap(x):
        other = pltpu.roll(x, BLK, axis=2)
        sub = iota((FIELDS, NBLK, LANES), 1)
        across = iota((FIELDS, NBLK, LANES), 2)
        even = lax.rem(sub, 2) == 0
        other = jnp.where(even, pltpu.roll(other, NBLK - 1, axis=1), pltpu.roll(other, 1, axis=1))
        return jnp.where(even == (across < BLK), x, other)

    def step(t, field, row_of_sums, then):
        hi, lo = split(wide(field))
        i_hi, i_lo = split(wide(turn(field, sign)))
        rows = jnp.concatenate([hi, i_hi, hi, i_hi, lo, i_lo], axis=0)
        if t == 0:
            for c in range(CHUNKS):
                pack(t, c, rows)
            row = row_of_sums()
            enter()
            start_sum(t, row)
            near = [i for i in range(1, space) if offsets[i][0] == 0 or offsets[i][1:] == (0, 0)]
            other = [i for i in range(1, space) if i not in near]
            send(t, near)
            pl.semaphore_wait(ready, lines - 1)
            send_halo(t, hi, lo)
            send(t, other[: space // 4])
            middle_sum(t)
            send(t, other[space // 4 :])
            prepare()
        else:
            pack(t, 0, rows)
            send(t, range(1, chunk))
            start_sum(t, row_of_sums())
            pack(t, 1, rows)
            send(t, range(chunk, 2 * chunk))
            send_halo(t, hi, lo)
            middle_sum(t)
            for c in range(2, CHUNKS):
                pack(t, c, rows)
                send(t, range(c * chunk, (c + 1) * chunk))
        flux(t, field, hi, lo)
        sums = arrived(t, 0) + arrived(t, 1)
        then()
        sums = sums + arrived(t, 2)
        sums = sums + arrived(t, 3)
        return own_part[...] + mortared(sums)

    hess = []
    gram = {}
    state = {}

    def gram_products(t):
        own = products([], vector.at[t], True)
        return own + (products([vector.at[i] for i in range(t)], vector.at[t], False) if t else [])

    def image_products(t):
        return products([vector.at[i] for i in range(t + 1)], images.at[t], True)

    def new_vector(t):
        number = 2 * (t + 1)
        sums = [two_sum(*pair) for pair in end_sum(t + 1, number + 2 + 2 * t)]
        gram[t, t] = (sums[number + 1][0] - 1.0) + sums[number + 1][1]
        for i in range(t):
            gram[i, t] = (sums[number + 2 + 2 * i][0], sums[number + 3 + 2 * i][0])
        value, lost = sums[number]
        factors = []
        for i in range(t + 1):
            for part in range(2):
                h, rest = sums[2 * i + part]
                whole = (h,) + halves(h)
                square, error = two_product(whole, whole)
                value, missed = two_sum(value, -square)
                lost = lost + (missed - error - 2.0 * h * rest + square * gram[i, i])
            factors.append((sums[2 * i][0], sums[2 * i + 1][0]))
        for k in range(t + 1):
            for i in range(k):
                (a, b), (c, d), (g, f) = factors[i], factors[k], gram[i, k]
                lost = lost + 2.0 * ((a * c + b * d) * g - (a * d - b * c) * f)
        length = jnp.sqrt(jnp.maximum(value + lost, 0.0) + EPS)
        rest = images[t]
        for i in range(t + 1):
            rest = minus(rest, factors[i], vector[i])
        hess.append((factors, length))
        return rest / length

    for copy in copies[5:6]:
        copy.wait()
    forcing = swap(field_ref[...])

    def first_vector():
        first = jnp.sqrt(end_sum(0, 1)[0][0] + EPS)
        state["first"] = first
        vector[0] = forcing / first
        state["gram"] = gram_products(0)

    plain = step(0, forcing, lambda: square_sum(forcing), first_vector)
    first = state["first"]
    images[0] = jnp.where(first < jnp.inf, plain / first, 0.0)

    for t in range(1, KRY):

        def sums(t=t):
            return packed_sums(image_products(t - 1) + state["gram"])

        def next_vector(t=t):
            vector[t] = new_vector(t - 1)
            state["gram"] = gram_products(t)

        plain = step(t, images[t - 1], sums, next_vector)
        factors, length = hess[t - 1]
        for i in range(t):
            plain = minus(plain, factors[i], images[i])
        images[t] = plain / length

    start_sum(KRY, packed_sums(image_products(KRY - 1) + state["gram"]))
    for t in range(KRY):
        out_ref[t] = swap(vector[t])
    middle_sum(KRY)
    out_ref[KRY] = swap(new_vector(KRY - 1))

    row = iota((2, KRY + 1), 0)
    column = iota((2, KRY + 1), 1)
    for j, (factors, length) in enumerate(hess):
        table = jnp.zeros((2, KRY + 1), F32)
        for index, factor in enumerate(factors):
            for part in range(2):
                table = jnp.where((row == part) & (column == index), factor[part], table)
        hess_ref[j] = jnp.where((row == 0) & (column == j + 1), length, table)

    for t in range(KRY):
        for side in range(2):
            halo_copy(t, side, halo_send).wait()
        for c in range(CHUNKS):
            wait_chunk(t, c, a2a_send)
    for r in range(KRY + 1):
        part = first_buf.at[r, pl.ds(0, LINE - 1)]
        pltpu.make_async_copy(part, part, red_send.at[r, 0]).wait()
        part = second_buf.at[r, pl.ds(0, wide_group - 1)]
        pltpu.make_async_copy(part, part, red_send.at[r, 1]).wait()


def solution(mesh):
    space, modes = mesh.shape["space"], mesh.shape["mode"]
    wide_group = space // LINE * modes
    sums = KRY + 1
    chunk = space // CHUNKS
    codes = np.array([(z * LINE + y * 2 + c) for z, y, c in sequence(space)], np.int32)
    codes = np.repeat(codes.reshape(CHUNKS, 1, chunk), 2, axis=1).reshape(2 * space, 1)
    dma = pltpu.SemaphoreType.DMA

    def local(right, jac, cols, halo, blocks, slot, target, phase, mortar):
        field = right[0].reshape(2, FIELDS, NBLK // 2, LANES).transpose(1, 2, 0, 3)
        field = field.reshape(FIELDS, NBLK, LANES)
        jac = jac.transpose(1, 2, 3, 0, 4).reshape(FIELDS**3, 2, NBLK)
        vmem = pl.BlockSpec(memory_space=pltpu.VMEM)
        basis, table = pl.pallas_call(
            functools.partial(kernel, space, modes),
            out_shape=(
                jax.ShapeDtypeStruct((KRY + 1, FIELDS, NBLK, LANES), F32),
                jax.ShapeDtypeStruct((KRY, 2, KRY + 1), F32),
            ),
            in_specs=[pl.BlockSpec(memory_space=pltpu.HBM)] * 10,
            out_specs=(vmem, vmem),
            scratch_shapes=[
                pltpu.VMEM((FIELDS, NBLK, LANES), F32),
                pltpu.VMEM((FIELDS**3, 2, NBLK), F32),
                pltpu.VMEM((FIELDS - 1, NBLK), jnp.int32),
                pltpu.VMEM((1, HB), jnp.int32),
                pltpu.VMEM((1, LANES), jnp.int32),
                pltpu.VMEM((1, LANES), jnp.int32),
                pltpu.VMEM((1, 2 * space), jnp.int32),
                pltpu.VMEM((1, LANES), jnp.int32),
                pltpu.VMEM((BLK, BLK), F32),
                pltpu.VMEM((2 * space, 1), jnp.int32),
                dma((10,)),
                pltpu.VMEM((KRY, space, ROW, LANES), F32),
                pltpu.VMEM((KRY, space, ROW, LANES), F32),
                pltpu.VMEM((KRY, FIELDS, HB, LANES), F32),
                pltpu.VMEM((KRY, 2, FIELDS, HB, LANES), F32),
                pltpu.VMEM((sums, LINE, 1, LANES), F32),
                pltpu.VMEM((sums, wide_group, 1, LANES), F32),
                pltpu.VMEM((FIELDS, NBLK // 8, 2 * FIELDS * FIELDS, 8, LANES), F32),
                pltpu.VMEM((CHUNKS, 2 * space // CHUNKS, 6 * NBLK), BF16),
                pltpu.VMEM((CHUNKS, NBLK, 4 * space // CHUNKS), BF16),
                pltpu.VMEM(((FIELDS - 1) * NBLK, 4 * NBLK), BF16),
                pltpu.VMEM((HB, 2 * NBLK), BF16),
                pltpu.VMEM((LANES, LANES), F32),
                pltpu.VMEM((2, FIELDS, FIELDS * NBLK, LANES), F32),
                pltpu.VMEM((FIELDS, NBLK, LANES), F32),
                pltpu.VMEM((KRY, FIELDS, NBLK, LANES), F32),
                pltpu.VMEM((KRY, FIELDS, NBLK, LANES), F32),
                pltpu.SemaphoreType.REGULAR,
                dma((KRY, CHUNKS)),
                dma((KRY, CHUNKS)),
                dma((KRY, 2)),
                dma((KRY, 2)),
                dma((sums, 2)),
                dma((sums, 2)),
            ],
            compiler_params=pltpu.CompilerParams(
                collective_id=0, has_side_effects=True, vmem_limit_bytes=64 << 20
            ),
        )(
            field,
            jac,
            cols,
            halo.reshape(1, HB),
            blocks.reshape(1, LANES),
            slot.reshape(1, LANES),
            target.reshape(1, 2 * space),
            phase,
            mortar,
            jnp.asarray(codes),
        )
        basis = basis.reshape(KRY + 1, FIELDS, NBLK // 2, 2, LANES).transpose(0, 3, 1, 2, 4)
        basis = basis.reshape(KRY + 1, 1, 2, FIELDS, NBLK * BLK)
        return basis, table.transpose(1, 2, 0)

    return jax.shard_map(
        local,
        mesh=mesh,
        in_specs=(
            P("mode", None, None, "space"),
            P(None, None, None, None, "space"),
            P(None, "space"),
            P("space"),
            P("space"),
            P("space"),
            P("space"),
            P("mode", "space"),
            P("space", None),
        ),
        out_specs=(P(None, "mode", None, None, "space"), P()),
        check_vma=False,
    )
```
